128 devices in a mesh: head: 16 (over z, y), tok: 8 (over x, core).
Axes of the slice: x: 4, y: 4, z: 4, core: 2. Of those that a mesh axis runs over, the one named last changes fastest.
Arguments:
- queries: bfloat16 [2048, 8192], P('tok', 'head'), may hold values from -6 to 6
- cache: bfloat16 [4, 4096, 256], P(None, 'tok'), may hold values from -6 to 6
- new_kv: bfloat16 [4, 2048, 256], P(None, 'tok'), may hold values from -6 to 6
- q_gain: float32 [128], replicated, may hold values from 0.5 to 2.2
- k_gain: float32 [128], replicated, may hold values from 0.5 to 2.2
- out_weight: bfloat16 [8192, 4096], P('head'), may hold values from -0.5 to 0.5
- residual: bfloat16 [2048, 4096], P(('tok', 'head')), may hold values from -3 to 3
- norm_gain: float32 [4096], replicated, may hold values from 0.25 to 1.75
- expert_ids: int32 [2048, 8], P(('tok', 'head')), may hold values from 0 to 127, all different within a row; in each aligned block of 16 rows (0 to 15, 16 to 31, ...) at most 2 rows name the same one
- combine_weight: bfloat16 [2048, 8], P(('tok', 'head')), may hold values from 0.049804688 to 0.5
- prefix_len: int32 [1], replicated, may hold values from 2048 to 4096
- w_gate_up: bfloat16 [128, 4096, 1536], P(('head', 'tok')), may hold values from -0.09375 to 0.09375
- w_down: bfloat16 [128, 768, 4096], P(('head', 'tok')), may hold values from -0.21875 to 0.21875
Outputs:
- layer_out: bfloat16 [2048, 4096], P(('tok', 'head'))
The draws below stay inside these ranges and needn't reach their ends.
Inputs may be any that keep to these rules, and one draw needn't show every extreme that they name: `expert_ids`: in each aligned block of 16 rows (the rows of one device) no expert is named by more than 2 rows, and some expert reaches 2.
All inputs are finite; a program needn't handle non-finite values.
Results may differ from the reference program's by a relative error of at most 0.022.
Values may be sent and summed in bfloat16 or wider, within the bound.
No kernel may reach another device: no remote copies, remote signals or barrier semaphores. Data moves between devices by JAX's collectives and lax.ppermute only.
A program may use at most 128 MiB of HBM per device.

```python
import math
import jax
import jax.numpy as jnp
import numpy as np
from jax import lax

D = 4096
HEADS = 64
KV_HEADS = 4
HD = 128
FFE = 768
TOPK = 8
ROWS_DEV = 16
TOKENS = 2048
PREFIX = 4096
EXPERTS = 128
CAP = 2


def steps_of(key, dims, split, smallest, high):
    level, own = 1.0, jax.random.fold_in(key, 6)
    for dim, blocks in split:
        heights = jnp.exp(jax.random.uniform(jax.random.fold_in(own, dim), (blocks,), jnp.float32, smallest / len(split), high / len(split)))
        level = level * jnp.repeat(heights, dims[dim] // blocks).reshape([-1 if axis == dim else 1 for axis in range(len(dims))])
    return level


def routed_block(key, own, number, rows, amount, top, most, skew):
    ranking = jax.random.permutation(key, amount)
    packed, common = shares(amount, rows * top, most, skew, True), shares(amount, rows * top, most, skew, False)
    places = jnp.arange(amount)

    def named(sizes, turn):
        used = int((sizes > 0).sum())
        fixed = max(1, used // 4)
        moved = fixed + (places - fixed + turn * (used - fixed)) % max(1, amount - fixed)
        return jnp.zeros((amount,), jnp.int32).at[ranking[jnp.where(places < fixed, places, moved)]].set(jnp.asarray(sizes, jnp.int32))

    sizes = jnp.where(number % 4 == 0, named(packed, number // 4), named(common, number - number // 4 - 1))
    mixed = jax.random.permutation(jax.random.fold_in(own, 3), amount)
    giver, sink = mixed[0:amount // 2 * 2:2], mixed[1:amount // 2 * 2:2]
    slack = jnp.minimum(sizes[giver] - 1, most - sizes[sink]) // 2
    slack = jnp.where((giver == ranking[0]) | (sink == ranking[0]) | (sizes[sink] == 0), 0, jnp.maximum(slack, 0))
    moved = jax.random.randint(jax.random.fold_in(own, 4), (amount // 2,), 0, 1 << 20) % (slack + 1)
    sizes = sizes.at[giver].add(-moved).at[sink].add(moved)
    items = jnp.searchsorted(jnp.cumsum(sizes), jnp.arange(rows * top), side="right").astype(jnp.int32)
    grid = items.reshape(top, rows).T
    grid = grid[jax.random.permutation(jax.random.fold_in(own, 1), rows)]
    turn = jax.random.randint(jax.random.fold_in(own, 2), (rows, 1), 0, top)
    return jnp.take_along_axis(grid, (jnp.arange(top)[None, :] + turn) % top, axis=1)


def shares(amount, total, bound, skew, full):
    weights = [(1 << 20) // math.isqrt(rank ** skew) + 1 for rank in range(1, amount + 1)]
    largest = bound if full else min(bound, max(-(-total // amount), total * weights[0] // sum(weights)))
    least = 1 if total - largest >= amount - 1 else 0
    holding, rest = [largest] + [least] * (amount - 1), total - largest - least * (amount - 1)
    while rest > 0:
        candidates = [i for i in range(1, amount) if holding[i] < largest] or [i for i in range(1, amount) if holding[i] < bound]
        pool, remaining = sum([weights[i] for i in candidates]), rest
        for i in candidates:
            extra = min(bound - holding[i], max(1, remaining * weights[i] // pool), rest)
            holding[i] = holding[i] + extra
            rest = rest - extra
    return np.array(holding)


def normal_values(key, extent, spread, bound, split=(), held_as=jnp.bfloat16):
    drawn = spread * jax.random.normal(key, extent, jnp.float32)
    if split:
        drawn = drawn * steps_of(key, extent, split, -0.22, 0.18)
    return jnp.clip(drawn, -bound, bound).astype(held_as)


def setup_inputs(seed: int = 0) -> dict:
    key_list = jax.random.split(jax.random.key(seed), 14)
    queries = normal_values(key_list[0], (TOKENS, HEADS * HD), 1.0, 6.0, ((0, 8), (1, 16)))
    cache = normal_values(key_list[1], (KV_HEADS, PREFIX, 2 * HD), 1.0, 6.0, ((1, 8),))
    new_kv = normal_values(key_list[2], (KV_HEADS, TOKENS, 2 * HD), 1.0, 6.0, ((1, 8),))
    q_gain = jnp.clip(jnp.exp(jax.random.uniform(key_list[3], (HD,), jnp.float32, math.log(0.5), math.log(2.2))), 0.5, 2.2)
    k_gain = jnp.clip(jnp.exp(jax.random.uniform(key_list[4], (HD,), jnp.float32, math.log(0.5), math.log(2.2))), 0.5, 2.2)
    out_weight = normal_values(key_list[5], (HEADS * HD, D), HD ** -0.5, 0.5, ((0, 16),))
    residual = normal_values(key_list[6], (TOKENS, D), 0.5, 3.0, ((0, 128),))
    norm_gain = jnp.clip(1.0 + 0.15 * jax.random.normal(key_list[7], (D,), jnp.float32), 0.25, 1.75)
    expert_ids_keys = jax.random.split(jax.random.fold_in(key_list[8], 1), TOKENS // ROWS_DEV)
    expert_ids_turns = jax.random.permutation(jax.random.fold_in(key_list[8], 3), TOKENS // ROWS_DEV)
    expert_ids = jax.vmap(lambda own, number: routed_block(jax.random.fold_in(key_list[8], 2), own, number, ROWS_DEV, EXPERTS, TOPK, CAP, 2))(expert_ids_keys, expert_ids_turns).reshape((TOKENS, TOPK))
    combine_weight = jnp.clip(jnp.exp(math.log(0.5) - 2.306499 * jax.random.uniform(key_list[9], (TOKENS, TOPK), jnp.float32) ** steps_of(key_list[9], (TOKENS, TOPK), ((0, 128),), -0.2, 0.2)), 0.049804688, 0.5).astype(jnp.bfloat16)
    prefix_len = jax.random.randint(key_list[10], (1,), PREFIX // 2, PREFIX + 1).astype(jnp.int32)
    w_gate_up = normal_values(key_list[11], (EXPERTS, D, 2 * FFE), D ** -0.5, 0.09375, ((0, 128),))
    w_down = normal_values(key_list[12], (EXPERTS, FFE, D), FFE ** -0.5, 0.21875, ((0, 128),))
    return {"queries": queries, "cache": cache, "new_kv": new_kv, "q_gain": q_gain, "k_gain": k_gain, "out_weight": out_weight, "residual": residual, "norm_gain": norm_gain, "expert_ids": expert_ids, "combine_weight": combine_weight, "prefix_len": prefix_len, "w_gate_up": w_gate_up, "w_down": w_down}


EPSILON = 1e-06

def rms_scale(values, gain):
    mean_square = lax.optimization_barrier(jnp.mean(values * values, axis=-1, keepdims=True))
    return values * lax.rsqrt(mean_square + EPSILON) * gain

def normed_block(block, k_gain):
    key_part = rms_scale(block[:, :HD].astype(jnp.float32), k_gain).astype(jnp.bfloat16)
    return jnp.concatenate([key_part, block[:, HD:]], axis=1)

def reference(queries, cache, new_kv, q_gain, k_gain, out_weight, residual, norm_gain, expert_ids, combine_weight, prefix_len, w_gate_up, w_down):
    group_size = HEADS // KV_HEADS
    query_all = rms_scale(queries.reshape(TOKENS, HEADS, HD).astype(jnp.float32), q_gain).astype(jnp.bfloat16)
    key_position = jnp.arange(PREFIX + TOKENS, dtype=jnp.int32)
    query_position = jnp.arange(TOKENS, dtype=jnp.int32)
    visible = jnp.where(key_position[None, :] < PREFIX, key_position[None, :] < prefix_len[0], key_position[None, :] - PREFIX <= query_position[:, None])

    def one_head(head_index):
        kv_head = head_index // group_size
        keyval = jnp.concatenate([lax.dynamic_index_in_dim(cache, kv_head, 0, keepdims=False), lax.dynamic_index_in_dim(new_kv, kv_head, 0, keepdims=False)], axis=0)
        keyval = normed_block(keyval, k_gain)
        query_head = lax.dynamic_index_in_dim(query_all, head_index, 1, keepdims=False)
        scores = jnp.dot(query_head, keyval[:, :HD].T, preferred_element_type=jnp.float32) * HD ** (-0.5)
        weights = jnp.where(visible, jnp.exp(scores), 0.0)
        total = lax.optimization_barrier(jnp.sum(weights, axis=1, keepdims=True))
        mixed = jnp.dot(weights.astype(jnp.bfloat16), keyval[:, HD:], preferred_element_type=jnp.float32)
        return (mixed / total).astype(jnp.bfloat16)
    per_head = lax.map(one_head, jnp.arange(HEADS, dtype=jnp.int32))
    attn = jnp.transpose(per_head, (1, 0, 2)).reshape(TOKENS, HEADS * HD)
    hidden = residual.astype(jnp.float32) + jnp.dot(attn, out_weight, preferred_element_type=jnp.float32)
    normed = rms_scale(hidden, norm_gain.astype(jnp.float32)).astype(jnp.bfloat16)
    blocks = TOKENS // ROWS_DEV
    flat_ids = expert_ids.reshape(blocks, ROWS_DEV * TOPK).astype(jnp.int32)
    onehot = (flat_ids[:, :, None] == jnp.arange(EXPERTS, dtype=jnp.int32)[None, None, :]).astype(jnp.int32)
    before = jnp.cumsum(onehot, axis=1) - onehot
    slot_index = lax.optimization_barrier(jnp.sum(before * onehot, axis=2)).astype(jnp.int32)
    token_index = jnp.repeat(jnp.arange(TOKENS, dtype=jnp.int32).reshape(blocks, ROWS_DEV), TOPK, axis=1)
    block_index = jnp.broadcast_to(jnp.arange(blocks, dtype=jnp.int32)[:, None], flat_ids.shape)
    table = jnp.full((EXPERTS, blocks, CAP), TOKENS, jnp.int32).at[flat_ids, block_index, slot_index].set(token_index)
    padded = jnp.concatenate([normed, jnp.zeros((1, D), jnp.bfloat16)], axis=0)

    def one_expert(expert_index):
        picked_rows = padded[table[expert_index].reshape(-1)]
        both = jnp.dot(picked_rows, w_gate_up[expert_index], preferred_element_type=jnp.float32)
        active = (jax.nn.silu(both[:, :FFE]) * both[:, FFE:]).astype(jnp.bfloat16)
        return jnp.dot(active, w_down[expert_index], preferred_element_type=jnp.float32).astype(jnp.bfloat16)
    outputs = lax.map(one_expert, jnp.arange(EXPERTS, dtype=jnp.int32))
    position = (block_index * CAP + slot_index).reshape(TOKENS, TOPK)
    gathered = outputs[flat_ids.reshape(TOKENS, TOPK), position]
    expert_sum = jnp.einsum('tk,tkd->td', combine_weight.astype(jnp.float32), gathered.astype(jnp.float32))
    return (hidden + expert_sum).astype(jnp.bfloat16)
```

```python
import functools
import math

import jax
import jax.numpy as jnp
from jax import lax
from jax.experimental import pallas as pl
from jax.experimental.pallas import tpu as pltpu
from jax.sharding import Mesh
from jax.sharding import PartitionSpec as P

HEADS = 64
KV_HEADS = 4
HD = 128
WIDTH = 4096
HALF = WIDTH // 2
ROWS = 16
QROWS = 256
QHEADS = 4
CACHE_ROWS = 512
SHARD = CACHE_ROWS + QROWS
SHARDS = 8
EXPERTS = 128
SLOTS = 2
CHUNKS = 8
PIECE = WIDTH // CHUNKS
LINES = CHUNKS * SLOTS
FFE = 768
GROUP = 16
GROUP_LINES = GROUP * LINES
EPSILON = 1e-06
SCALE = math.log2(math.e) / math.sqrt(HD)
MB = 1 << 20

F32 = jnp.float32
BF16 = jnp.bfloat16

VMEM = functools.partial(pl.BlockSpec, memory_space=pltpu.VMEM)
SMEM = functools.partial(pl.BlockSpec, memory_space=pltpu.SMEM)
ANY = functools.partial(pl.BlockSpec, memory_space=pl.ANY)


def params(limit):
    return pltpu.CompilerParams(vmem_limit_bytes=limit * MB)


def rms_scale(values, gain):
    mean_square = jnp.mean(values * values, axis=-1, keepdims=True)
    return values * lax.rsqrt(mean_square + EPSILON) * gain


def shift(step):
    return [(i, (i + step) % 4) for i in range(4)]


def prep_kernel(kv_ref, cache_ref, new_ref, gain_ref, out_ref):
    for ref, start, rows in ((cache_ref, 0, CACHE_ROWS), (new_ref, CACHE_ROWS, QROWS)):
        keys = rms_scale(ref[:, :HD].astype(F32), gain_ref[...]).astype(BF16)
        out_ref[pl.ds(start, rows), :HD] = keys
        out_ref[pl.ds(start, rows), HD:] = ref[:, HD:]


def prep(kv_index, cache, new_kv, k_gain):
    return pl.pallas_call(
        prep_kernel,
        grid_spec=pltpu.PrefetchScalarGridSpec(
            num_scalar_prefetch=1,
            grid=(1,),
            in_specs=[
                pl.BlockSpec((None, CACHE_ROWS, 2 * HD), lambda i, kv: (kv[0], 0, 0)),
                pl.BlockSpec((None, QROWS, 2 * HD), lambda i, kv: (kv[0], 0, 0)),
                pl.BlockSpec((1, HD), lambda i, kv: (0, 0)),
            ],
            out_specs=pl.BlockSpec((SHARD, 2 * HD), lambda i, kv: (0, 0)),
        ),
        out_shape=jax.ShapeDtypeStruct((SHARD, 2 * HD), BF16),
        compiler_params=params(8),
    )(kv_index, cache, new_kv, k_gain)


def attention_kernel(
    place_ref, q_ref, gain_ref, *rest
):
    shards, rest = rest[:SHARDS], rest[SHARDS:]
    weight_ref, rest = rest[0], rest[1:]
    out_a, out_b, rest = rest[:4], rest[4:8], rest[8:]
    qn, kv, weight, acc, total, attn, result, kv_sem, weight_sem = rest
    limit, z, y, x, c = (place_ref[i] for i in range(5))
    tok = x * 2 + c
    copies = []
    for i in range(SHARDS):
        core = c if i < 4 else 1 - c
        owner = ((x + 4 - i % 4) % 4) * 2 + core
        copies.append(pltpu.make_async_copy(shards[i], kv.at[owner], kv_sem.at[i]))
    weight_copy = pltpu.make_async_copy(weight_ref, weight, weight_sem)
    for copy in copies:
        copy.start()
    weight_copy.start()
    for h in range(QHEADS):
        head = q_ref[:, h * HD : (h + 1) * HD].astype(F32)
        qn[pl.ds(h * QROWS, QROWS), :] = rms_scale(head, gain_ref[...]).astype(BF16)
    acc[...] = jnp.zeros_like(acc)
    total[...] = jnp.zeros_like(total)
    for copy in copies:
        copy.wait()

    def block(owner, start, rows, mask):
        keys = kv[owner, pl.ds(start, rows), :HD]
        values = kv[owner, pl.ds(start, rows), HD:]
        for h in range(QHEADS):
            at = pl.ds(h * QROWS, QROWS)
            scores = lax.dot_general(
                qn[at, :], keys, (((1,), (1,)), ((), ())), preferred_element_type=F32
            )
            weights = jnp.exp2(scores * SCALE)
            if mask is not None:
                weights = jnp.where(mask, weights, 0.0)
            part = weights[:, :HD]
            for i in range(1, rows // HD):
                part = part + weights[:, i * HD : (i + 1) * HD]
            total[at, :] += part
            acc[at, :] += jnp.dot(weights.astype(BF16), values, preferred_element_type=F32)

    full = limit // CACHE_ROWS

    @pl.loop(0, full)
    def _(owner):
        block(owner, 0, CACHE_ROWS, None)

    @pl.when(limit % CACHE_ROWS != 0)
    def _():
        position = lax.broadcasted_iota(jnp.int32, (QROWS, CACHE_ROWS), 1) + full * CACHE_ROWS
        block(full, 0, CACHE_ROWS, position < limit)

    @pl.loop(0, tok)
    def _(owner):
        block(owner, CACHE_ROWS, QROWS, None)

    key = lax.broadcasted_iota(jnp.int32, (QROWS, QROWS), 1)
    query = lax.broadcasted_iota(jnp.int32, (QROWS, QROWS), 0)
    block(tok, CACHE_ROWS, QROWS, key <= query)

    for h in range(QHEADS):
        at = pl.ds(h * QROWS, QROWS)
        whole = jnp.sum(total[at, :], axis=1, keepdims=True)
        attn[:, h * HD : (h + 1) * HD] = (acc[at, :] / whole).astype(BF16)
    weight_copy.wait()
    for n in range(8):
        columns = slice(n * 512, (n + 1) * 512)
        product = jnp.dot(attn[...], weight[:, columns], preferred_element_type=F32)
        result[:, :, columns] = product.astype(BF16).reshape(16, ROWS, 512)
    for k in range(4):
        for i in range(4):
            out_a[k][i] = result[i * 4 + (y + k) % 4, :, :HALF]
            out_b[k][i] = result[((z + k) % 4) * 4 + i, :, HALF:]


def attention(place, queries, q_gain, shards, weight):
    part = jax.ShapeDtypeStruct((4, ROWS, HALF), BF16)
    return pl.pallas_call(
        attention_kernel,
        in_specs=[SMEM(), VMEM(), VMEM()] + [ANY()] * (SHARDS + 1),
        out_specs=[VMEM()] * 8,
        out_shape=[part] * 8,
        scratch_shapes=[
            pltpu.VMEM((QHEADS * QROWS, HD), BF16),
            pltpu.VMEM((SHARDS, SHARD, 2 * HD), BF16),
            pltpu.VMEM((QHEADS * HD, WIDTH), BF16),
            pltpu.VMEM((QHEADS * QROWS, HD), F32),
            pltpu.VMEM((QHEADS * QROWS, HD), F32),
            pltpu.VMEM((QROWS, QHEADS * HD), BF16),
            pltpu.VMEM((16, ROWS, WIDTH), BF16),
            pltpu.SemaphoreType.DMA((SHARDS,)),
            pltpu.SemaphoreType.DMA,
        ],
        compiler_params=params(28),
    )(place, queries, q_gain, *shards, weight)


def sum_kernel(place_ref, *refs):
    parts_a, parts_b, refs = refs[:4], refs[4:8], refs[8:]
    out_a, out_b, (held_a, held_b) = refs[:4], refs[4:8], refs[8:]
    z, y = place_ref[1], place_ref[2]
    for parts, held in ((parts_a, held_a), (parts_b, held_b)):
        for i in range(4):
            value = parts[0][i].astype(F32)
            for other in parts[1:]:
                value = value + other[i].astype(F32)
            held[i] = value.astype(BF16)
    for k in range(4):
        out_a[k][...] = held_a[(z + k) % 4]
        out_b[k][...] = held_b[(y + k) % 4]


def first_sum(place, parts):
    row = jax.ShapeDtypeStruct((ROWS, HALF), BF16)
    return pl.pallas_call(
        sum_kernel,
        in_specs=[SMEM()] + [VMEM()] * 8,
        out_specs=[VMEM()] * 8,
        out_shape=[row] * 8,
        scratch_shapes=[pltpu.VMEM((4, ROWS, HALF), BF16)] * 2,
        compiler_params=params(12),
    )(place, *parts)


def route_kernel(columns_ref, rows_ref, mix_ref, placing_ref, mixing_ref):
    line = lax.broadcasted_iota(jnp.int32, (EXPERTS * LINES, EXPERTS), 0)
    lane = lax.broadcasted_iota(jnp.int32, (EXPERTS * LINES, EXPERTS), 1)
    slot = (line // LINES) * SLOTS + line % SLOTS
    hit = slot == columns_ref[0:1, :]
    for k in range(1, 8):
        hit = hit | (slot == columns_ref[k : k + 1, :])
    hit = hit & ((line // SLOTS) % CHUNKS == lane // ROWS)
    placing_ref[...] = jnp.where(hit, 1.0, 0.0).astype(BF16)
    line = lax.broadcasted_iota(jnp.int32, (EXPERTS, EXPERTS * LINES), 1)
    row = lax.broadcasted_iota(jnp.int32, (EXPERTS, EXPERTS * LINES), 0)
    slot = (line // LINES) * SLOTS + line % SLOTS
    value = jnp.zeros(slot.shape, F32)
    for k in range(8):
        value = jnp.where(slot == rows_ref[:, k : k + 1], mix_ref[:, k : k + 1], value)
    same = (line // SLOTS) % CHUNKS == row // ROWS
    mixing_ref[...] = jnp.where(same, value, 0.0).astype(BF16)


def route(expert_ids, combine_weight):
    flat = expert_ids.reshape(-1)
    index = jnp.arange(flat.shape[0], dtype=jnp.int32)
    earlier = (flat[:, None] == flat[None, :]) & (index[None, :] < index[:, None])
    slot = jnp.sum(earlier.astype(jnp.int32), axis=1)
    target = (flat * SLOTS + slot).reshape(expert_ids.shape)
    return pl.pallas_call(
        route_kernel,
        in_specs=[VMEM()] * 3,
        out_specs=[VMEM()] * 2,
        out_shape=[
            jax.ShapeDtypeStruct((EXPERTS * LINES, EXPERTS), BF16),
            jax.ShapeDtypeStruct((EXPERTS, EXPERTS * LINES), BF16),
        ],
        compiler_params=params(12),
    )(
        jnp.tile(target.T, (1, CHUNKS)),
        jnp.tile(target, (CHUNKS, 1)),
        jnp.tile(combine_weight.astype(F32), (CHUNKS, 1)),
    )


def dispatch_kernel(*refs):
    parts_a, parts_b, refs = refs[:4], refs[4:8], refs[8:]
    residual_ref, gain_ref, placing_ref, hidden_ref, out_ref, pieces = refs
    for parts, start in ((parts_a, 0), (parts_b, HALF)):
        value = parts[0][...].astype(F32)
        for other in parts[1:]:
            value = value + other[...].astype(F32)
        columns = slice(start, start + HALF)
        hidden_ref[:, columns] = residual_ref[:, columns].astype(F32) + value
    normed = rms_scale(hidden_ref[...], gain_ref[...]).astype(BF16)
    for k in range(CHUNKS):
        pieces[pl.ds(k * ROWS, ROWS), :] = normed[:, k * PIECE : (k + 1) * PIECE]
    for g in range(8):
        lines = jnp.dot(
            placing_ref[pl.ds(g * GROUP_LINES, GROUP_LINES), :],
            pieces[...],
            preferred_element_type=F32,
        )
        out_ref[pl.ds(g * GROUP, GROUP)] = lines.astype(BF16).reshape(GROUP, LINES, PIECE)


def dispatch(parts, residual, norm_gain, placing):
    return pl.pallas_call(
        dispatch_kernel,
        in_specs=[VMEM()] * 11,
        out_specs=[VMEM()] * 2,
        out_shape=[
            jax.ShapeDtypeStruct((ROWS, WIDTH), F32),
            jax.ShapeDtypeStruct((EXPERTS, LINES, PIECE), BF16),
        ],
        scratch_shapes=[pltpu.VMEM((EXPERTS, PIECE), BF16)],
        compiler_params=params(12),
    )(*parts, residual, norm_gain, placing)


def expert_kernel(lines_ref, up_ref, down_ref, out_ref, rows, both, active, back):
    size = (GROUP_LINES, GROUP_LINES)
    first = lax.broadcasted_iota(jnp.int32, size, 0)
    second = lax.broadcasted_iota(jnp.int32, size, 1)
    span = GROUP * SLOTS

    def held(by_chunk, by_source):
        source = (by_chunk % span) // SLOTS
        line = source * LINES + (by_chunk // span) * SLOTS + by_chunk % SLOTS
        return jnp.where(line == by_source, 1.0, 0.0).astype(BF16)

    gather, scatter = held(first, second), held(second, first)
    for g in range(8):
        group = lines_ref[pl.ds(g * GROUP, GROUP)].reshape(GROUP_LINES, PIECE)
        sorted_lines = jnp.dot(gather, group, preferred_element_type=F32).astype(BF16)
        for k in range(CHUNKS):
            rows[pl.ds(g * span, span), k * PIECE : (k + 1) * PIECE] = sorted_lines[
                k * span : (k + 1) * span, :
            ]
    for n in range(2 * FFE // 256):
        columns = slice(n * 256, (n + 1) * 256)
        both[:, columns] = jnp.dot(rows[...], up_ref[:, columns], preferred_element_type=F32)
    gate = both[:, :FFE]
    active[...] = (gate * jax.nn.sigmoid(gate) * both[:, FFE:]).astype(BF16)
    for k in range(CHUNKS):
        columns = slice(k * PIECE, (k + 1) * PIECE)
        down = jnp.dot(active[...], down_ref[:, columns], preferred_element_type=F32)
        down = down.astype(BF16)
        for g in range(8):
            back[g, pl.ds(k * span, span), :] = down[g * span : (g + 1) * span, :]
    for g in range(8):
        lines = jnp.dot(scatter, back[g], preferred_element_type=F32).astype(BF16)
        out_ref[pl.ds(g * GROUP, GROUP)] = lines.reshape(GROUP, LINES, PIECE)


def experts(lines, gate_up, down):
    return pl.pallas_call(
        expert_kernel,
        in_specs=[VMEM()] * 3,
        out_specs=VMEM(),
        out_shape=jax.ShapeDtypeStruct((EXPERTS, LINES, PIECE), BF16),
        scratch_shapes=[
            pltpu.VMEM((EXPERTS * SLOTS, WIDTH), BF16),
            pltpu.VMEM((EXPERTS * SLOTS, 2 * FFE), F32),
            pltpu.VMEM((EXPERTS * SLOTS, FFE), BF16),
            pltpu.VMEM((8, GROUP_LINES, PIECE), BF16),
        ],
        compiler_params=params(40),
    )(lines, gate_up, down)


def combine_kernel(lines_ref, mixing_ref, hidden_ref, out_ref):
    lines = lines_ref[...].reshape(EXPERTS * LINES, PIECE)
    mixed = jnp.dot(mixing_ref[...], lines, preferred_element_type=F32)
    for k in range(CHUNKS):
        columns = slice(k * PIECE, (k + 1) * PIECE)
        value = hidden_ref[:, columns] + mixed[k * ROWS : (k + 1) * ROWS, :]
        out_ref[:, columns] = value.astype(BF16)


def combine(lines, mixing, hidden):
    return pl.pallas_call(
        combine_kernel,
        in_specs=[VMEM()] * 3,
        out_specs=VMEM(),
        out_shape=jax.ShapeDtypeStruct((ROWS, WIDTH), BF16),
        compiler_params=params(12),
    )(lines, mixing, hidden)


def per_device(
    queries,
    cache,
    new_kv,
    q_gain,
    k_gain,
    out_weight,
    residual,
    norm_gain,
    expert_ids,
    combine_weight,
    prefix_len,
    w_gate_up,
    w_down,
):
    z, y, x, c = (lax.axis_index(name).astype(jnp.int32) for name in ("z", "y", "x", "c"))
    place = jnp.stack([prefix_len[0], z, y, x, c])
    own = prep(z.reshape(1), cache, new_kv, k_gain.reshape(1, HD))
    swap = functools.partial(lax.ppermute, axis_name="c", perm=[(0, 1), (1, 0)])
    near = [own] + [lax.ppermute(own, "x", shift(k)) for k in (1, 2, 3)]
    shards = near + [swap(shard) for shard in near]
    placing, mixing = route(expert_ids, combine_weight)
    queries, placing, mixing = lax.optimization_barrier((queries, placing, mixing))
    parts = attention(place, queries, q_gain.reshape(1, HD), shards, out_weight)
    part_a = [parts[0]] + [lax.ppermute(parts[k], "y", shift(k)) for k in (1, 2, 3)]
    part_b = [parts[4]] + [lax.ppermute(parts[4 + k], "z", shift(k)) for k in (1, 2, 3)]
    parts = first_sum(place, part_a + part_b)
    part_a = [parts[0]] + [lax.ppermute(parts[k], "z", shift(k)) for k in (1, 2, 3)]
    part_b = [parts[4]] + [lax.ppermute(parts[4 + k], "y", shift(k)) for k in (1, 2, 3)]
    hidden, lines = dispatch(
        part_a + part_b, residual, norm_gain.reshape(1, WIDTH), placing
    )
    everyone = ("z", "y", "x", "c")
    lines = lax.all_to_all(lines, everyone, split_axis=0, concat_axis=0, tiled=True)
    lines = experts(lines, w_gate_up[0], w_down[0])
    lines = lax.all_to_all(lines, everyone, split_axis=0, concat_axis=0, tiled=True)
    return combine(lines, mixing, hidden)


def solution(mesh):
    fine = Mesh(mesh.devices.reshape(4, 4, 4, 2), ("z", "y", "x", "c"))
    head, tok = ("z", "y"), ("x", "c")
    placed = (
        P(tok, head),
        P(None, tok, None),
        P(None, tok, None),
        P(),
        P(),
        P(head, None),
        P(tok + head, None),
        P(),
        P(tok + head, None),
        P(tok + head, None),
        P(),
        P(head + tok, None, None),
        P(head + tok, None, None),
    )
    return jax.shard_map(
        per_device, mesh=fine, in_specs=placed, out_specs=P(tok + head, None), check_vma=False
    )
```

```python
import functools
import math

import jax
import jax.numpy as jnp
from jax import lax
from jax.experimental import pallas as pl
from jax.experimental.pallas import tpu as pltpu
from jax.sharding import Mesh
from jax.sharding import PartitionSpec as P

HEADS = 64
KV_HEADS = 4
HD = 128
WIDTH = 4096
ROWS = 16
QROWS = 256
QHEADS = 4
CACHE_ROWS = 512
SHARD = CACHE_ROWS + QROWS
GROUPS = 16
EXPERTS = 128
SLOTS = 2
CHUNKS = 8
PIECE = WIDTH // CHUNKS
LINES = CHUNKS * SLOTS
FFE = 768
GROUP = 16
GROUP_LINES = GROUP * LINES
EPSILON = 1e-06
SCALE = math.log2(math.e) / math.sqrt(HD)
MB = 1 << 20

F32 = jnp.float32
BF16 = jnp.bfloat16

VMEM = functools.partial(pl.BlockSpec, memory_space=pltpu.VMEM)
SMEM = functools.partial(pl.BlockSpec, memory_space=pltpu.SMEM)
HBM = functools.partial(pl.BlockSpec, memory_space=pltpu.HBM)


def params(limit):
    return pltpu.CompilerParams(vmem_limit_bytes=limit * MB)


def rms_scale(values, gain):
    mean_square = jnp.mean(values * values, axis=-1, keepdims=True)
    return values * lax.rsqrt(mean_square + EPSILON) * gain


def shift(step):
    return [(i, (i + step) % 4) for i in range(4)]


def prep_kernel(place_ref, cache_ref, new_ref, gain_ref, out_ref, cache, new, sems):
    head = place_ref[1]
    copies = (
        pltpu.make_async_copy(cache_ref.at[head], cache, sems.at[0]),
        pltpu.make_async_copy(new_ref.at[head], new, sems.at[1]),
    )
    for copy in copies:
        copy.start()
    for copy, ref, start, rows in (
        (copies[1], new, CACHE_ROWS, QROWS),
        (copies[0], cache, 0, CACHE_ROWS),
    ):
        copy.wait()
        keys = rms_scale(ref[:, :HD].astype(F32), gain_ref[...]).astype(BF16)
        out_ref[pl.ds(start, rows), :HD] = keys
        out_ref[pl.ds(start, rows), HD:] = ref[:, HD:]


def prep(place, cache, new_kv, k_gain):
    return pl.pallas_call(
        prep_kernel,
        in_specs=[SMEM(), HBM(), HBM(), VMEM()],
        out_specs=VMEM(),
        out_shape=jax.ShapeDtypeStruct((SHARD, 2 * HD), BF16),
        scratch_shapes=[
            pltpu.VMEM((CACHE_ROWS, 2 * HD), BF16),
            pltpu.VMEM((QROWS, 2 * HD), BF16),
            pltpu.SemaphoreType.DMA((2,)),
        ],
        compiler_params=params(8),
    )(place, cache, new_kv, k_gain)


def seen_blocks(place_ref, core_offset, distances, shards, qn, acc, total):
    limit, x, c = place_ref[0], place_ref[3], place_ref[4]
    core = lax.rem(c + core_offset, 2)
    tok = x * 2 + c

    def block(ref, start, rows, mask):
        keys = ref[pl.ds(start, rows), :HD]
        values = ref[pl.ds(start, rows), HD:]
        scores = lax.dot_general(
            qn[...], keys, (((1,), (1,)), ((), ())), preferred_element_type=F32
        )
        weights = jnp.exp2(scores * SCALE)
        if mask is not None:
            weights = jnp.where(mask, weights, 0.0)
        part = weights[:, :HD]
        for i in range(1, rows // HD):
            part = part + weights[:, i * HD : (i + 1) * HD]
        total[...] += part
        acc[...] += jnp.dot(weights.astype(BF16), values, preferred_element_type=F32)

    for distance, ref in zip(distances, shards):
        owner = lax.rem(x + 4 - distance, 4) * 2 + core
        visible = limit - owner * CACHE_ROWS

        @pl.when(visible >= CACHE_ROWS)
        def _():
            block(ref, 0, CACHE_ROWS, None)

        @pl.when((visible > 0) & (visible < CACHE_ROWS))
        def _():
            key = lax.broadcasted_iota(jnp.int32, (QHEADS * QROWS, CACHE_ROWS), 1)
            block(ref, 0, CACHE_ROWS, key < visible)

        if distance == 0 and core_offset == 0:
            key = lax.broadcasted_iota(jnp.int32, (QHEADS * QROWS, QROWS), 1)
            query = lax.broadcasted_iota(jnp.int32, (QHEADS * QROWS, QROWS), 0)
            block(ref, CACHE_ROWS, QROWS, key <= lax.rem(query, QROWS))
        else:

            @pl.when(owner < tok)
            def _():
                block(ref, CACHE_ROWS, QROWS, None)


def near_kernel(place_ref, q_ref, gain_ref, own_ref, other_ref, qn, acc, total):
    for h in range(QHEADS):
        head = q_ref[:, h * HD : (h + 1) * HD].astype(F32)
        qn[pl.ds(h * QROWS, QROWS), :] = rms_scale(head, gain_ref[...]).astype(BF16)
    acc[...] = jnp.zeros_like(acc)
    total[...] = jnp.zeros_like(total)
    seen_blocks(place_ref, 0, (0,), (own_ref,), qn, acc, total)
    seen_blocks(place_ref, 1, (0,), (other_ref,), qn, acc, total)


STATE = (
    jax.ShapeDtypeStruct((QHEADS * QROWS, HD), F32),
    jax.ShapeDtypeStruct((QHEADS * QROWS, HD), F32),
)


def attend_near(place, queries, q_gain, own, other):
    return pl.pallas_call(
        near_kernel,
        in_specs=[SMEM()] + [VMEM()] * 4,
        out_specs=[VMEM()] * 3,
        out_shape=[jax.ShapeDtypeStruct((QHEADS * QROWS, HD), BF16), *STATE],
        compiler_params=params(16),
    )(place, queries, q_gain, own, other)


def far_kernel(place_ref, qn, acc_ref, total_ref, first, second, third, acc, total):
    acc[...] = acc_ref[...]
    total[...] = total_ref[...]
    seen_blocks(place_ref, 0, (1, 2, 3), (first, second, third), qn, acc, total)


def attend_far(place, qn, acc, total, shards):
    return pl.pallas_call(
        far_kernel,
        in_specs=[SMEM()] + [VMEM()] * 6,
        out_specs=[VMEM()] * 2,
        out_shape=list(STATE),
        compiler_params=params(16),
    )(place, qn, acc, total, *shards)


def last_kernel(
    place_ref, qn, acc_ref, total_ref, first, second, third, weight_ref, out_ref, acc, total, attn,
    weight, sem,
):
    copy = pltpu.make_async_copy(weight_ref, weight, sem)
    copy.start()
    acc[...] = acc_ref[...]
    total[...] = total_ref[...]
    seen_blocks(place_ref, 1, (1, 2, 3), (first, second, third), qn, acc, total)
    for h in range(QHEADS):
        at = pl.ds(h * QROWS, QROWS)
        whole = jnp.sum(total[at, :], axis=1, keepdims=True)
        attn[:, h * HD : (h + 1) * HD] = (acc[at, :] / whole).astype(BF16)
    copy.wait()
    for n in range(8):
        columns = slice(n * 512, (n + 1) * 512)
        product = jnp.dot(attn[...], weight[:, columns], preferred_element_type=F32)
        out_ref[:, :, columns] = product.astype(BF16).reshape(GROUPS, ROWS, 512)


def attend_last(place, qn, acc, total, shards, weight):
    return pl.pallas_call(
        last_kernel,
        in_specs=[SMEM()] + [VMEM()] * 6 + [HBM()],
        out_specs=VMEM(),
        out_shape=jax.ShapeDtypeStruct((GROUPS, ROWS, WIDTH), BF16),
        scratch_shapes=[
            pltpu.VMEM((QHEADS * QROWS, HD), F32),
            pltpu.VMEM((QHEADS * QROWS, HD), F32),
            pltpu.VMEM((QROWS, QHEADS * HD), BF16),
            pltpu.VMEM((QHEADS * HD, WIDTH), BF16),
            pltpu.SemaphoreType.DMA,
        ],
        compiler_params=params(20),
    )(place, qn, acc, total, *shards, weight)


def route_kernel(columns_ref, rows_ref, mix_ref, placing_ref, mixing_ref):
    line = lax.broadcasted_iota(jnp.int32, (EXPERTS * LINES, EXPERTS), 0)
    lane = lax.broadcasted_iota(jnp.int32, (EXPERTS * LINES, EXPERTS), 1)
    slot = (line // LINES) * SLOTS + line % SLOTS
    hit = slot == columns_ref[0:1, :]
    for k in range(1, 8):
        hit = hit | (slot == columns_ref[k : k + 1, :])
    hit = hit & ((line // SLOTS) % CHUNKS == lane // ROWS)
    placing_ref[...] = jnp.where(hit, 1.0, 0.0).astype(BF16)
    line = lax.broadcasted_iota(jnp.int32, (EXPERTS, EXPERTS * LINES), 1)
    row = lax.broadcasted_iota(jnp.int32, (EXPERTS, EXPERTS * LINES), 0)
    slot = (line // LINES) * SLOTS + line % SLOTS
    value = jnp.zeros(slot.shape, F32)
    for k in range(8):
        value = jnp.where(slot == rows_ref[:, k : k + 1], mix_ref[:, k : k + 1], value)
    same = (line // SLOTS) % CHUNKS == row // ROWS
    mixing_ref[...] = jnp.where(same, value, 0.0).astype(BF16)


def route(expert_ids, combine_weight):
    flat = expert_ids.reshape(-1)
    index = jnp.arange(flat.shape[0], dtype=jnp.int32)
    earlier = (flat[:, None] == flat[None, :]) & (index[None, :] < index[:, None])
    slot = jnp.sum(earlier.astype(jnp.int32), axis=1)
    target = (flat * SLOTS + slot).reshape(expert_ids.shape)
    return pl.pallas_call(
        route_kernel,
        in_specs=[VMEM()] * 3,
        out_specs=[VMEM()] * 2,
        out_shape=[
            jax.ShapeDtypeStruct((EXPERTS * LINES, EXPERTS), BF16),
            jax.ShapeDtypeStruct((EXPERTS, EXPERTS * LINES), BF16),
        ],
        compiler_params=params(12),
    )(
        jnp.tile(target.T, (1, CHUNKS)),
        jnp.tile(target, (CHUNKS, 1)),
        jnp.tile(combine_weight.astype(F32), (CHUNKS, 1)),
    )


def dispatch_kernel(parts_ref, residual_ref, gain_ref, placing_ref, hidden_ref, out_ref, pieces):
    for n in range(8):
        columns = slice(n * 512, (n + 1) * 512)
        value = residual_ref[:, columns].astype(F32)
        for g in range(GROUPS):
            value = value + parts_ref[g, :, columns].astype(F32)
        hidden_ref[:, columns] = value
    normed = rms_scale(hidden_ref[...], gain_ref[...]).astype(BF16)
    for k in range(CHUNKS):
        pieces[pl.ds(k * ROWS, ROWS), :] = normed[:, k * PIECE : (k + 1) * PIECE]
    for g in range(8):
        lines = jnp.dot(
            placing_ref[pl.ds(g * GROUP_LINES, GROUP_LINES), :],
            pieces[...],
            preferred_element_type=F32,
        )
        out_ref[pl.ds(g * GROUP, GROUP)] = lines.astype(BF16).reshape(GROUP, LINES, PIECE)


def dispatch(parts, residual, norm_gain, placing):
    return pl.pallas_call(
        dispatch_kernel,
        in_specs=[VMEM()] * 4,
        out_specs=[VMEM()] * 2,
        out_shape=[
            jax.ShapeDtypeStruct((ROWS, WIDTH), F32),
            jax.ShapeDtypeStruct((EXPERTS, LINES, PIECE), BF16),
        ],
        scratch_shapes=[pltpu.VMEM((EXPERTS, PIECE), BF16)],
        compiler_params=params(12),
    )(parts, residual, norm_gain, placing)


def expert_kernel(
    lines_ref, up_ref, down_hbm, out_ref, rows, both, active, back, down_ref, sem
):
    copy = pltpu.make_async_copy(down_hbm, down_ref, sem)
    copy.start()
    size = (GROUP_LINES, GROUP_LINES)
    first = lax.broadcasted_iota(jnp.int32, size, 0)
    second = lax.broadcasted_iota(jnp.int32, size, 1)
    span = GROUP * SLOTS

    def held(by_chunk, by_source):
        source = (by_chunk % span) // SLOTS
        line = source * LINES + (by_chunk // span) * SLOTS + by_chunk % SLOTS
        return jnp.where(line == by_source, 1.0, 0.0).astype(BF16)

    gather, scatter = held(first, second), held(second, first)
    for g in range(8):
        group = lines_ref[pl.ds(g * GROUP, GROUP)].reshape(GROUP_LINES, PIECE)
        sorted_lines = jnp.dot(gather, group, preferred_element_type=F32).astype(BF16)
        for k in range(CHUNKS):
            rows[pl.ds(g * span, span), k * PIECE : (k + 1) * PIECE] = sorted_lines[
                k * span : (k + 1) * span, :
            ]
    for n in range(2 * FFE // 256):
        columns = slice(n * 256, (n + 1) * 256)
        both[:, columns] = jnp.dot(rows[...], up_ref[:, columns], preferred_element_type=F32)
    gate = both[:, :FFE]
    active[...] = (gate * jax.nn.sigmoid(gate) * both[:, FFE:]).astype(BF16)
    copy.wait()
    for k in range(CHUNKS):
        columns = slice(k * PIECE, (k + 1) * PIECE)
        down = jnp.dot(active[...], down_ref[:, columns], preferred_element_type=F32)
        down = down.astype(BF16)
        for g in range(8):
            back[g, pl.ds(k * span, span), :] = down[g * span : (g + 1) * span, :]
    for g in range(8):
        lines = jnp.dot(scatter, back[g], preferred_element_type=F32).astype(BF16)
        out_ref[pl.ds(g * GROUP, GROUP)] = lines.reshape(GROUP, LINES, PIECE)


def experts(lines, gate_up, down):
    return pl.pallas_call(
        expert_kernel,
        in_specs=[VMEM(), VMEM(), HBM()],
        out_specs=VMEM(),
        out_shape=jax.ShapeDtypeStruct((EXPERTS, LINES, PIECE), BF16),
        scratch_shapes=[
            pltpu.VMEM((EXPERTS * SLOTS, WIDTH), BF16),
            pltpu.VMEM((EXPERTS * SLOTS, 2 * FFE), F32),
            pltpu.VMEM((EXPERTS * SLOTS, FFE), BF16),
            pltpu.VMEM((8, GROUP_LINES, PIECE), BF16),
            pltpu.VMEM((FFE, WIDTH), BF16),
            pltpu.SemaphoreType.DMA,
        ],
        compiler_params=params(24),
    )(lines, gate_up, down)


def combine_kernel(lines_ref, mixing_ref, hidden_ref, out_ref):
    lines = lines_ref[...].reshape(EXPERTS * LINES, PIECE)
    mixed = jnp.dot(mixing_ref[...], lines, preferred_element_type=F32)
    for k in range(CHUNKS):
        columns = slice(k * PIECE, (k + 1) * PIECE)
        value = hidden_ref[:, columns] + mixed[k * ROWS : (k + 1) * ROWS, :]
        out_ref[:, columns] = value.astype(BF16)


def combine(lines, mixing, hidden):
    return pl.pallas_call(
        combine_kernel,
        in_specs=[VMEM()] * 3,
        out_specs=VMEM(),
        out_shape=jax.ShapeDtypeStruct((ROWS, WIDTH), BF16),
        compiler_params=params(12),
    )(lines, mixing, hidden)


def per_device(
    queries,
    cache,
    new_kv,
    q_gain,
    k_gain,
    out_weight,
    residual,
    norm_gain,
    expert_ids,
    combine_weight,
    prefix_len,
    w_gate_up,
    w_down,
):
    z, y, x, c = (lax.axis_index(name).astype(jnp.int32) for name in ("z", "y", "x", "c"))
    place = jnp.stack([prefix_len[0], z, y, x, c])
    held = functools.partial(pltpu.with_memory_space_constraint, memory_space=pltpu.HBM)
    own = prep(place, held(cache), held(new_kv), k_gain.reshape(1, HD))
    swap = functools.partial(lax.ppermute, axis_name="c", perm=[(0, 1), (1, 0)])
    other = swap(own)
    near = [lax.ppermute(own, "x", shift(k)) for k in (1, 2, 3)]
    placing, mixing = route(expert_ids, combine_weight)
    queries, placing, mixing = lax.optimization_barrier((queries, placing, mixing))
    qn, acc, total = attend_near(place, queries, q_gain.reshape(1, HD), own, other)
    *near, qn, acc, total = lax.optimization_barrier((*near, qn, acc, total))
    far = [swap(shard) for shard in near]
    acc, total = attend_far(place, qn, acc, total, near)
    parts = attend_last(place, qn, acc, total, far, held(out_weight))
    parts = lax.all_to_all(parts, ("z", "y"), split_axis=0, concat_axis=0, tiled=True)
    hidden, lines = dispatch(parts, residual, norm_gain.reshape(1, WIDTH), placing)
    everyone = ("z", "y", "x", "c")
    lines = lax.all_to_all(lines, everyone, split_axis=0, concat_axis=0, tiled=True)
    lines = experts(lines, w_gate_up[0], w_down[0])
    lines = lax.all_to_all(lines, everyone, split_axis=0, concat_axis=0, tiled=True)
    return combine(lines, mixing, hidden)


def solution(mesh):
    fine = Mesh(mesh.devices.reshape(4, 4, 4, 2), ("z", "y", "x", "c"))
    head, tok = ("z", "y"), ("x", "c")
    placed = (
        P(tok, head),
        P(None, tok, None),
        P(None, tok, None),
        P(),
        P(),
        P(head, None),
        P(tok + head, None),
        P(),
        P(tok + head, None),
        P(tok + head, None),
        P(),
        P(head + tok, None, None),
        P(head + tok, None, None),
    )
    return jax.shard_map(
        per_device, mesh=fine, in_specs=placed, out_specs=P(tok + head, None), check_vma=False
    )
```

```python
import functools
import math

import jax
import jax.numpy as jnp
from jax import lax
from jax.experimental import pallas as pl
from jax.experimental.pallas import tpu as pltpu
from jax.sharding import Mesh
from jax.sharding import PartitionSpec as P

HEADS = 64
KV_HEADS = 4
HD = 128
WIDTH = 4096
ROWS = 16
QROWS = 256
QHEADS = 4
CACHE_ROWS = 512
SHARD = CACHE_ROWS + QROWS
GROUPS = 16
EXPERTS = 128
SLOTS = 2
CHUNKS = 8
PIECE = WIDTH // CHUNKS
LINES = CHUNKS * SLOTS
FFE = 768
GROUP = 16
GROUP_LINES = GROUP * LINES
EPSILON = 1e-06
SCALE = math.log2(math.e) / math.sqrt(HD)
MB = 1 << 20

F32 = jnp.float32
BF16 = jnp.bfloat16

VMEM = functools.partial(pl.BlockSpec, memory_space=pltpu.VMEM)
SMEM = functools.partial(pl.BlockSpec, memory_space=pltpu.SMEM)
HBM = functools.partial(pl.BlockSpec, memory_space=pltpu.HBM)


def params(limit):
    return pltpu.CompilerParams(vmem_limit_bytes=limit * MB)


def rms_scale(values, gain):
    mean_square = jnp.mean(values * values, axis=-1, keepdims=True)
    return values * lax.rsqrt(mean_square + EPSILON) * gain


def shift(step):
    return [(i, (i + step) % 4) for i in range(4)]


def prep_kernel(
    place_ref, cache_ref, new_ref, gain_ref, out_ref, part_ref, cache, new, gain, sems
):
    head, quarter = place_ref[1], place_ref[2]
    copies = (
        pltpu.make_async_copy(gain_ref, gain, sems.at[0]),
        pltpu.make_async_copy(new_ref.at[head], new, sems.at[1]),
        pltpu.make_async_copy(cache_ref.at[head], cache, sems.at[2]),
    )
    for copy in copies:
        copy.start()
    copies[0].wait()
    for copy, ref, start, rows in (
        (copies[1], new, CACHE_ROWS, QROWS),
        (copies[2], cache, 0, CACHE_ROWS),
    ):
        copy.wait()
        keys = rms_scale(ref[:, :HD].astype(F32), gain[...]).astype(BF16)
        out_ref[pl.ds(start, rows), :HD] = keys
        out_ref[pl.ds(start, rows), HD:] = ref[:, HD:]
    for start, there, rows in quarter_rows(quarter):
        part_ref[pl.ds(there, rows), :] = out_ref[pl.ds(start, rows), :]


def quarter_rows(quarter):
    cache_rows, new_rows = CACHE_ROWS // 4, QROWS // 4
    return (
        (pl.multiple_of(quarter * cache_rows, cache_rows), 0, cache_rows),
        (pl.multiple_of(CACHE_ROWS + quarter * new_rows, new_rows), cache_rows, new_rows),
    )


def prep(place, cache, new_kv, k_gain):
    return pl.pallas_call(
        prep_kernel,
        in_specs=[SMEM(), HBM(), HBM(), HBM()],
        out_specs=[VMEM()] * 2,
        out_shape=[
            jax.ShapeDtypeStruct((SHARD, 2 * HD), BF16),
            jax.ShapeDtypeStruct((SHARD // 4, 2 * HD), BF16),
        ],
        scratch_shapes=[
            pltpu.VMEM((CACHE_ROWS, 2 * HD), BF16),
            pltpu.VMEM((QROWS, 2 * HD), BF16),
            pltpu.VMEM((1, HD), F32),
            pltpu.SemaphoreType.DMA((3,)),
        ],
        compiler_params=params(8),
    )(place, cache, new_kv, k_gain)


def join(place_ref, parts, whole):
    y = place_ref[2]
    for k, part in enumerate(parts):
        for start, there, rows in quarter_rows(lax.rem(y + 4 - k, 4)):
            whole[pl.ds(start, rows), :] = part[pl.ds(there, rows), :]


def seen_blocks(place_ref, core_offset, distances, shards, qn, acc, total):
    limit, x, c = place_ref[0], place_ref[3], place_ref[4]
    core = lax.rem(c + core_offset, 2)
    tok = x * 2 + c

    def block(ref, start, rows, mask):
        keys = ref[pl.ds(start, rows), :HD]
        values = ref[pl.ds(start, rows), HD:]
        scores = lax.dot_general(
            qn[...], keys, (((1,), (1,)), ((), ())), preferred_element_type=F32
        )
        weights = jnp.exp2(scores * SCALE)
        if mask is not None:
            weights = jnp.where(mask, weights, 0.0)
        part = weights[:, :HD]
        for i in range(1, rows // HD):
            part = part + weights[:, i * HD : (i + 1) * HD]
        total[...] += part
        acc[...] += jnp.dot(weights.astype(BF16), values, preferred_element_type=F32)

    for distance, ref in zip(distances, shards):
        owner = lax.rem(x + 4 - distance, 4) * 2 + core
        visible = limit - owner * CACHE_ROWS

        @pl.when(visible >= CACHE_ROWS)
        def _():
            block(ref, 0, CACHE_ROWS, None)

        @pl.when((visible > 0) & (visible < CACHE_ROWS))
        def _():
            key = lax.broadcasted_iota(jnp.int32, (QHEADS * QROWS, CACHE_ROWS), 1)
            block(ref, 0, CACHE_ROWS, key < visible)

        if distance == 0 and core_offset == 0:
            key = lax.broadcasted_iota(jnp.int32, (QHEADS * QROWS, QROWS), 1)
            query = lax.broadcasted_iota(jnp.int32, (QHEADS * QROWS, QROWS), 0)
            block(ref, CACHE_ROWS, QROWS, key <= lax.rem(query, QROWS))
        else:

            @pl.when(owner < tok)
            def _():
                block(ref, CACHE_ROWS, QROWS, None)


def near_kernel(place_ref, qn, own_ref, other_ref, acc, total):
    acc[...] = jnp.zeros_like(acc)
    total[...] = jnp.zeros_like(total)
    seen_blocks(place_ref, 0, (0,), (own_ref,), qn, acc, total)
    seen_blocks(place_ref, 1, (0,), (other_ref,), qn, acc, total)


STATE = (
    jax.ShapeDtypeStruct((QHEADS * QROWS, HD), F32),
    jax.ShapeDtypeStruct((QHEADS * QROWS, HD), F32),
)


def attend_near(place, qn, own, other):
    return pl.pallas_call(
        near_kernel,
        in_specs=[SMEM()] + [VMEM()] * 3,
        out_specs=[VMEM()] * 2,
        out_shape=list(STATE),
        compiler_params=params(16),
    )(place, qn, own, other)


def far_kernel(place_ref, qn, acc_ref, total_ref, *refs):
    first, third, parts, (acc, total, second) = refs[0], refs[1], refs[2:6], refs[6:]
    acc[...] = acc_ref[...]
    total[...] = total_ref[...]
    join(place_ref, parts, second)
    seen_blocks(place_ref, 0, (1, 3, 2), (first, third, second), qn, acc, total)


def attend_far(place, qn, acc, total, shards):
    return pl.pallas_call(
        far_kernel,
        in_specs=[SMEM()] + [VMEM()] * 9,
        out_specs=[VMEM()] * 2,
        out_shape=list(STATE),
        scratch_shapes=[pltpu.VMEM((SHARD, 2 * HD), BF16)],
        compiler_params=params(16),
    )(place, qn, acc, total, *shards)


def last_kernel(place_ref, qn, acc_ref, total_ref, *refs):
    first, third, parts, refs = refs[0], refs[1], refs[2:6], refs[6:]
    weight_ref, out_ref, acc, total, attn, weight, second, sem = refs
    copy = pltpu.make_async_copy(weight_ref, weight, sem)
    copy.start()
    acc[...] = acc_ref[...]
    total[...] = total_ref[...]
    join(place_ref, parts, second)
    seen_blocks(place_ref, 1, (1, 3, 2), (first, third, second), qn, acc, total)
    for h in range(QHEADS):
        at = pl.ds(h * QROWS, QROWS)
        whole = jnp.sum(total[at, :], axis=1, keepdims=True)
        attn[:, h * HD : (h + 1) * HD] = (acc[at, :] / whole).astype(BF16)
    copy.wait()
    for n in range(8):
        columns = slice(n * 512, (n + 1) * 512)
        product = jnp.dot(attn[...], weight[:, columns], preferred_element_type=F32)
        out_ref[:, :, columns] = product.astype(BF16).reshape(GROUPS, ROWS, 512)


def attend_last(place, qn, acc, total, shards, weight):
    return pl.pallas_call(
        last_kernel,
        in_specs=[SMEM()] + [VMEM()] * 9 + [HBM()],
        out_specs=VMEM(),
        out_shape=jax.ShapeDtypeStruct((GROUPS, ROWS, WIDTH), BF16),
        scratch_shapes=[
            pltpu.VMEM((QHEADS * QROWS, HD), F32),
            pltpu.VMEM((QHEADS * QROWS, HD), F32),
            pltpu.VMEM((QROWS, QHEADS * HD), BF16),
            pltpu.VMEM((QHEADS * HD, WIDTH), BF16),
            pltpu.VMEM((SHARD, 2 * HD), BF16),
            pltpu.SemaphoreType.DMA,
        ],
        compiler_params=params(20),
    )(place, qn, acc, total, *shards, weight)


def route_kernel(
    ids_hbm, weights_hbm, q_ref, gain_ref, placing_ref, mixing_ref, qn,
    ids_ref, weights_ref, queries, gain, sems,
):
    pairs = ((gain_ref, gain), (q_ref, queries), (ids_hbm, ids_ref), (weights_hbm, weights_ref))
    copies = [pltpu.make_async_copy(a, b, sems.at[i]) for i, (a, b) in enumerate(pairs)]
    for copy in copies:
        copy.start()
    for copy in copies:
        copy.wait()
    square = (EXPERTS, EXPERTS)
    expert = lax.broadcasted_iota(jnp.int32, square, 0)
    lane = lax.broadcasted_iota(jnp.int32, square, 1)
    row = lax.broadcasted_iota(jnp.int32, (ROWS, EXPERTS), 0)
    spread = lax.broadcasted_iota(jnp.int32, (ROWS, EXPERTS), 1) % ROWS == row
    spread = jnp.where(spread, 1.0, 0.0).astype(BF16)
    ids = jnp.dot(ids_ref[...].astype(F32).astype(BF16), spread, preferred_element_type=F32)
    ids = ids.astype(jnp.int32)
    weights = jnp.dot(weights_ref[...], spread, preferred_element_type=F32)
    named = jnp.zeros(square, F32)
    value = jnp.zeros(square, F32)
    for k in range(8):
        hit = expert == ids[k : k + 1, :]
        named = jnp.where(hit, 1.0, named)
        value = jnp.where(hit, weights[k : k + 1, :], value)
    earlier = (expert // ROWS == lane // ROWS) & (expert < lane)
    before = jnp.dot(
        named.astype(BF16), jnp.where(earlier, 1.0, 0.0).astype(BF16), preferred_element_type=F32
    )
    lines = (EXPERTS * LINES, EXPERTS)
    line = lax.broadcasted_iota(jnp.int32, lines, 0)
    column = lax.broadcasted_iota(jnp.int32, lines, 1)
    same = (line // SLOTS) % CHUNKS == column // ROWS
    of_expert = line // LINES == column
    for out_ref, held in ((placing_ref, named), (mixing_ref, value)):
        table = jnp.zeros(lines, F32)
        for s in range(SLOTS):
            pick = jnp.where(of_expert & (line % SLOTS == s), 1.0, 0.0).astype(BF16)
            slot = jnp.where(before == s, held, 0.0).astype(BF16)
            table = table + jnp.dot(pick, slot, preferred_element_type=F32)
        out_ref[...] = jnp.where(same, table, 0.0).astype(BF16)
    for h in range(QHEADS):
        head = queries[:, h * HD : (h + 1) * HD].astype(F32)
        qn[pl.ds(h * QROWS, QROWS), :] = rms_scale(head, gain[...]).astype(BF16)


def route(expert_ids, combine_weight, queries, q_gain):
    return pl.pallas_call(
        route_kernel,
        in_specs=[HBM()] * 4,
        out_specs=[VMEM()] * 3,
        out_shape=[jax.ShapeDtypeStruct((EXPERTS * LINES, EXPERTS), BF16)] * 2
        + [jax.ShapeDtypeStruct((QHEADS * QROWS, HD), BF16)],
        scratch_shapes=[
            pltpu.VMEM((8, ROWS), jnp.int32),
            pltpu.VMEM((8, ROWS), BF16),
            pltpu.VMEM((QROWS, QHEADS * HD), BF16),
            pltpu.VMEM((1, HD), F32),
            pltpu.SemaphoreType.DMA((4,)),
        ],
        compiler_params=params(16),
    )(expert_ids, combine_weight, queries, q_gain)


def dispatch_kernel(parts_ref, residual_ref, gain_ref, placing_ref, hidden_ref, out_ref, pieces):
    for n in range(8):
        columns = slice(n * 512, (n + 1) * 512)
        value = residual_ref[:, columns].astype(F32)
        for g in range(GROUPS):
            value = value + parts_ref[g, :, columns].astype(F32)
        hidden_ref[:, columns] = value
    normed = rms_scale(hidden_ref[...], gain_ref[...]).astype(BF16)
    for k in range(CHUNKS):
        pieces[pl.ds(k * ROWS, ROWS), :] = normed[:, k * PIECE : (k + 1) * PIECE]
    for g in range(8):
        lines = jnp.dot(
            placing_ref[pl.ds(g * GROUP_LINES, GROUP_LINES), :],
            pieces[...],
            preferred_element_type=F32,
        )
        out_ref[pl.ds(g * GROUP, GROUP)] = lines.astype(BF16).reshape(GROUP, LINES, PIECE)


def dispatch(parts, residual, norm_gain, placing):
    return pl.pallas_call(
        dispatch_kernel,
        in_specs=[VMEM()] * 4,
        out_specs=[VMEM()] * 2,
        out_shape=[
            jax.ShapeDtypeStruct((ROWS, WIDTH), F32),
            jax.ShapeDtypeStruct((EXPERTS, LINES, PIECE), BF16),
        ],
        scratch_shapes=[pltpu.VMEM((EXPERTS, PIECE), BF16)],
        compiler_params=params(12),
    )(parts, residual, norm_gain, placing)


def expert_kernel(
    lines_ref, up_ref, down_hbm, out_ref, rows, both, active, back, down_ref, sem
):
    copy = pltpu.make_async_copy(down_hbm, down_ref, sem)
    copy.start()
    size = (GROUP_LINES, GROUP_LINES)
    first = lax.broadcasted_iota(jnp.int32, size, 0)
    second = lax.broadcasted_iota(jnp.int32, size, 1)
    span = GROUP * SLOTS

    def held(by_chunk, by_source):
        source = (by_chunk % span) // SLOTS
        line = source * LINES + (by_chunk // span) * SLOTS + by_chunk % SLOTS
        return jnp.where(line == by_source, 1.0, 0.0).astype(BF16)

    gather, scatter = held(first, second), held(second, first)
    for g in range(8):
        group = lines_ref[pl.ds(g * GROUP, GROUP)].reshape(GROUP_LINES, PIECE)
        sorted_lines = jnp.dot(gather, group, preferred_element_type=F32).astype(BF16)
        for k in range(CHUNKS):
            rows[pl.ds(g * span, span), k * PIECE : (k + 1) * PIECE] = sorted_lines[
                k * span : (k + 1) * span, :
            ]
    for n in range(2 * FFE // 256):
        columns = slice(n * 256, (n + 1) * 256)
        both[:, columns] = jnp.dot(rows[...], up_ref[:, columns], preferred_element_type=F32)
    gate = both[:, :FFE]
    active[...] = (gate * jax.nn.sigmoid(gate) * both[:, FFE:]).astype(BF16)
    copy.wait()
    for k in range(CHUNKS):
        columns = slice(k * PIECE, (k + 1) * PIECE)
        down = jnp.dot(active[...], down_ref[:, columns], preferred_element_type=F32)
        down = down.astype(BF16)
        for g in range(8):
            back[g, pl.ds(k * span, span), :] = down[g * span : (g + 1) * span, :]
    for g in range(8):
        lines = jnp.dot(scatter, back[g], preferred_element_type=F32).astype(BF16)
        out_ref[pl.ds(g * GROUP, GROUP)] = lines.reshape(GROUP, LINES, PIECE)


def experts(lines, gate_up, down):
    return pl.pallas_call(
        expert_kernel,
        in_specs=[VMEM(), VMEM(), HBM()],
        out_specs=VMEM(),
        out_shape=jax.ShapeDtypeStruct((EXPERTS, LINES, PIECE), BF16),
        scratch_shapes=[
            pltpu.VMEM((EXPERTS * SLOTS, WIDTH), BF16),
            pltpu.VMEM((EXPERTS * SLOTS, 2 * FFE), F32),
            pltpu.VMEM((EXPERTS * SLOTS, FFE), BF16),
            pltpu.VMEM((8, GROUP_LINES, PIECE), BF16),
            pltpu.VMEM((FFE, WIDTH), BF16),
            pltpu.SemaphoreType.DMA,
        ],
        compiler_params=params(24),
    )(lines, gate_up, down)


def combine_kernel(lines_ref, mixing_ref, hidden_ref, out_ref):
    lines = lines_ref[...].reshape(EXPERTS * LINES, PIECE)
    mixed = lax.dot_general(
        mixing_ref[...], lines, (((0,), (0,)), ((), ())), preferred_element_type=F32
    )
    for k in range(CHUNKS):
        columns = slice(k * PIECE, (k + 1) * PIECE)
        value = hidden_ref[:, columns] + mixed[k * ROWS : (k + 1) * ROWS, :]
        out_ref[:, columns] = value.astype(BF16)


def combine(lines, mixing, hidden):
    return pl.pallas_call(
        combine_kernel,
        in_specs=[VMEM()] * 3,
        out_specs=VMEM(),
        out_shape=jax.ShapeDtypeStruct((ROWS, WIDTH), BF16),
        compiler_params=params(12),
    )(lines, mixing, hidden)


def per_device(
    queries,
    cache,
    new_kv,
    q_gain,
    k_gain,
    out_weight,
    residual,
    norm_gain,
    expert_ids,
    combine_weight,
    prefix_len,
    w_gate_up,
    w_down,
):
    z, y, x, c = (lax.axis_index(name).astype(jnp.int32) for name in ("z", "y", "x", "c"))
    place = jnp.stack([prefix_len[0], z, y, x, c])
    held = functools.partial(pltpu.with_memory_space_constraint, memory_space=pltpu.HBM)
    own, part = prep(place, held(cache), held(new_kv), held(k_gain.reshape(1, HD)))
    swap = functools.partial(lax.ppermute, axis_name="c", perm=[(0, 1), (1, 0)])
    other = swap(own)
    parts = [lax.ppermute(part, "x", shift(2))]
    placing, mixing, qn = route(
        held(expert_ids.T), held(combine_weight.T), held(queries), held(q_gain.reshape(1, HD))
    )
    whole, parts[0], placing, mixing, qn = lax.optimization_barrier(
        (own, parts[0], placing, mixing, qn)
    )
    part = swap(parts[0])
    near = [lax.ppermute(whole, "x", shift(k)) for k in (1, 3)]
    parts += [lax.ppermute(parts[0], "y", shift(k)) for k in (1, 2, 3)]
    acc, total = attend_near(place, qn, own, other)
    near = near + parts
    *near, qn, acc, total = lax.optimization_barrier((*near, qn, acc, total))
    far = [swap(near[0]), swap(near[1]), part] + [swap(shard) for shard in near[3:]]
    acc, total = attend_far(place, qn, acc, total, near)
    parts = attend_last(place, qn, acc, total, far, held(out_weight))
    parts = lax.all_to_all(parts, ("z", "y"), split_axis=0, concat_axis=0, tiled=True)
    hidden, lines = dispatch(parts, residual, norm_gain.reshape(1, WIDTH), placing)
    everyone = ("z", "y", "x", "c")
    lines = lax.all_to_all(lines, everyone, split_axis=0, concat_axis=0, tiled=True)
    lines = experts(lines, w_gate_up[0], w_down[0])
    lines = lax.all_to_all(lines, everyone, split_axis=0, concat_axis=0, tiled=True)
    return combine(lines, mixing, hidden)


def solution(mesh):
    fine = Mesh(mesh.devices.reshape(4, 4, 4, 2), ("z", "y", "x", "c"))
    head, tok = ("z", "y"), ("x", "c")
    placed = (
        P(tok, head),
        P(None, tok, None),
        P(None, tok, None),
        P(),
        P(),
        P(head, None),
        P(tok + head, None),
        P(),
        P(tok + head, None),
        P(tok + head, None),
        P(),
        P(head + tok, None, None),
        P(head + tok, None, None),
    )
    return jax.shard_map(
        per_device, mesh=fine, in_specs=placed, out_specs=P(tok + head, None), check_vma=False
    )
```

```python
import functools
import math

import jax
import jax.numpy as jnp
from jax import lax
from jax.experimental import pallas as pl
from jax.experimental.pallas import tpu as pltpu
from jax.sharding import Mesh
from jax.sharding import PartitionSpec as P

HEADS = 64
KV_HEADS = 4
HD = 128
WIDTH = 4096
ROWS = 16
QROWS = 256
QHEADS = 4
CACHE_ROWS = 512
SHARD = CACHE_ROWS + QROWS
PART = SHARD // 2
GROUPS = 16
EXPERTS = 128
SLOTS = 2
CHUNKS = 8
PIECE = WIDTH // CHUNKS
LINES = CHUNKS * SLOTS
FFE = 768
GROUP = 16
GROUP_LINES = GROUP * LINES
EPSILON = 1e-06
SCALE = math.log2(math.e) / math.sqrt(HD)
MB = 1 << 20

F32 = jnp.float32
BF16 = jnp.bfloat16

VMEM = functools.partial(pl.BlockSpec, memory_space=pltpu.VMEM)
SMEM = functools.partial(pl.BlockSpec, memory_space=pltpu.SMEM)
HBM = functools.partial(pl.BlockSpec, memory_space=pltpu.HBM)


def params(limit):
    return pltpu.CompilerParams(vmem_limit_bytes=limit * MB)


def rms_scale(values, gain):
    mean_square = jnp.mean(values * values, axis=-1, keepdims=True)
    return values * lax.rsqrt(mean_square + EPSILON) * gain


def shift(step):
    return [(i, (i + step) % 4) for i in range(4)]


def prep_kernel(place_ref, cache_ref, new_ref, gain_ref, first, second, cache, new, gain, sems):
    head = place_ref[1]
    copies = (
        pltpu.make_async_copy(gain_ref, gain, sems.at[0]),
        pltpu.make_async_copy(cache_ref.at[head], cache, sems.at[1]),
        pltpu.make_async_copy(new_ref.at[head], new, sems.at[2]),
    )
    for copy in copies:
        copy.start()
    for copy in copies:
        copy.wait()
    rest = CACHE_ROWS - PART
    for ref, start, out_ref, there, rows in (
        (cache, 0, first, 0, PART),
        (cache, PART, second, 0, rest),
        (new, 0, second, rest, QROWS),
    ):
        held = ref[pl.ds(start, rows), :]
        keys = rms_scale(held[:, :HD].astype(F32), gain[...]).astype(BF16)
        out_ref[pl.ds(there, rows), :HD] = keys
        out_ref[pl.ds(there, rows), HD:] = held[:, HD:]


def prep(place, cache, new_kv, k_gain):
    return pl.pallas_call(
        prep_kernel,
        in_specs=[SMEM(), HBM(), HBM(), HBM()],
        out_specs=[VMEM()] * 2,
        out_shape=[jax.ShapeDtypeStruct((PART, 2 * HD), BF16)] * 2,
        scratch_shapes=[
            pltpu.VMEM((CACHE_ROWS, 2 * HD), BF16),
            pltpu.VMEM((QROWS, 2 * HD), BF16),
            pltpu.VMEM((1, HD), F32),
            pltpu.SemaphoreType.DMA((3,)),
        ],
        compiler_params=params(8),
    )(place, cache, new_kv, k_gain)


def join(first, second, whole):
    whole[pl.ds(0, PART), :] = first[...]
    whole[pl.ds(PART, PART), :] = second[...]


def seen_blocks(limit, x, c, own, distances, shards, qn, acc, total):
    def block(ref, start, rows, mask=None):
        keys = ref[pl.ds(start, rows), :HD]
        values = ref[pl.ds(start, rows), HD:]
        scores = lax.dot_general(
            qn[...], keys, (((1,), (1,)), ((), ())), preferred_element_type=F32
        )
        weights = jnp.exp2(scores * SCALE)
        if mask is not None:
            weights = jnp.where(mask, weights, 0.0)
        part = weights[:, :HD]
        for i in range(1, rows // HD):
            part = part + weights[:, i * HD : (i + 1) * HD]
        total[...] += part
        acc[...] += jnp.dot(weights.astype(BF16), values, preferred_element_type=F32)

    tok = x * 2 + (c if own else 1 - c)
    for distance, ref in zip(distances, shards):
        owner = lax.rem(x + 4 - distance, 4) * 2 + c
        visible = limit - owner * CACHE_ROWS
        whole, earlier = visible >= CACHE_ROWS, owner < tok

        @pl.when(whole & earlier)
        def _():
            block(ref, 0, SHARD)

        @pl.when(whole & jnp.logical_not(earlier))
        def _():
            block(ref, 0, CACHE_ROWS)

        @pl.when((visible > 0) & (visible < CACHE_ROWS))
        def _():
            key = lax.broadcasted_iota(jnp.int32, (QHEADS * QROWS, CACHE_ROWS), 1)
            block(ref, 0, CACHE_ROWS, key < visible)

        @pl.when(jnp.logical_not(whole) & earlier)
        def _():
            block(ref, CACHE_ROWS, QROWS)

        if own and distance == 0:
            key = lax.broadcasted_iota(jnp.int32, (QHEADS * QROWS, QROWS), 1)
            query = lax.broadcasted_iota(jnp.int32, (QHEADS * QROWS, QROWS), 0)
            block(ref, CACHE_ROWS, QROWS, key <= lax.rem(query, QROWS))


STATE = jax.ShapeDtypeStruct((QHEADS * QROWS, HD), F32)
WHOLE = pltpu.VMEM((SHARD, 2 * HD), BF16)


def near_kernel(
    place_ref, qn, qn_other, first, second, weight_ref,
    acc, total, acc_other, total_other, weight, shard, sem,
):
    copy = pltpu.make_async_copy(weight_ref, weight, sem)
    copy.start()
    limit, x, c = place_ref[0], place_ref[3], place_ref[4]
    join(first, second, shard)
    for ref in (acc, total, acc_other, total_other):
        ref[...] = jnp.zeros_like(ref)
    seen_blocks(limit, x, c, False, (0,), (shard,), qn_other, acc_other, total_other)
    seen_blocks(limit, x, c, True, (0,), (shard,), qn, acc, total)
    copy.wait()


def attend_near(place, qn, qn_other, first, second, weight):
    return pl.pallas_call(
        near_kernel,
        in_specs=[SMEM()] + [VMEM()] * 4 + [HBM()],
        out_specs=[VMEM()] * 5,
        out_shape=[STATE] * 4 + [jax.ShapeDtypeStruct(weight.shape, BF16)],
        scratch_shapes=[WHOLE, pltpu.SemaphoreType.DMA],
        compiler_params=params(20),
    )(place, qn, qn_other, first, second, weight)


def middle_kernel(place_ref, qn, qn_other, *refs):
    before, parts, after, shards = refs[:4], refs[4:8], refs[8:12], refs[12:]
    limit, x, c = place_ref[0], place_ref[3], place_ref[4]
    for ref, out_ref in zip(before, after):
        out_ref[...] = ref[...]
    join(parts[0], parts[1], shards[0])
    join(parts[2], parts[3], shards[1])
    seen_blocks(limit, x, c, False, (1, 3), shards, qn_other, after[2], after[3])
    seen_blocks(limit, x, c, True, (1, 3), shards, qn, after[0], after[1])


def attend_middle(place, qn, qn_other, state, parts):
    return pl.pallas_call(
        middle_kernel,
        in_specs=[SMEM()] + [VMEM()] * 10,
        out_specs=[VMEM()] * 4,
        out_shape=[STATE] * 4,
        scratch_shapes=[WHOLE] * 2,
        compiler_params=params(16),
    )(place, qn, qn_other, *state, *parts)


def far_kernel(own, place_ref, qn, acc_ref, total_ref, first, second, out_ref, acc, total, shard):
    limit, x, c = place_ref[0], place_ref[3], place_ref[4]
    acc[...] = acc_ref[...]
    total[...] = total_ref[...]
    join(first, second, shard)
    seen_blocks(limit, x, c, own, (2,), (shard,), qn, acc, total)
    out_ref[:, :HD] = acc[...]
    out_ref[:, HD:] = total[...]


def attend_far(own, place, qn, acc, total, first, second):
    return pl.pallas_call(
        functools.partial(far_kernel, own),
        in_specs=[SMEM()] + [VMEM()] * 5,
        out_specs=VMEM(),
        out_shape=jax.ShapeDtypeStruct((QHEADS * QROWS, 2 * HD), F32),
        scratch_shapes=[
            pltpu.VMEM((QHEADS * QROWS, HD), F32),
            pltpu.VMEM((QHEADS * QROWS, HD), F32),
            WHOLE,
        ],
        compiler_params=params(16),
    )(place, qn, acc, total, first, second)


def project_kernel(own_ref, other_ref, weight, out_ref, attn):
    for h in range(QHEADS):
        at = pl.ds(h * QROWS, QROWS)
        both = own_ref[at, :] + other_ref[at, :]
        whole = jnp.sum(both[:, HD:], axis=1, keepdims=True)
        attn[:, h * HD : (h + 1) * HD] = (both[:, :HD] / whole).astype(BF16)
    for n in range(8):
        part = slice(n * 512, (n + 1) * 512)
        product = jnp.dot(attn[...], weight[:, part], preferred_element_type=F32)
        out_ref[:, :, part] = product.astype(BF16).reshape(GROUPS, ROWS, 512)


def project(own, other, weight):
    return pl.pallas_call(
        project_kernel,
        in_specs=[VMEM()] * 3,
        out_specs=VMEM(),
        out_shape=jax.ShapeDtypeStruct((GROUPS, ROWS, WIDTH), BF16),
        scratch_shapes=[pltpu.VMEM((QROWS, QHEADS * HD), BF16)],
        compiler_params=params(16),
    )(own, other, weight)


def route_kernel(
    ids_hbm, weights_hbm, q_ref, gain_ref, other_ref, placing_ref, mixing_ref, qn, qn_other,
    ids_ref, weights_ref, queries, gain, sems,
):
    pairs = ((gain_ref, gain), (q_ref, queries), (ids_hbm, ids_ref), (weights_hbm, weights_ref))
    copies = [pltpu.make_async_copy(a, b, sems.at[i]) for i, (a, b) in enumerate(pairs)]
    for copy in copies:
        copy.start()
    for copy in copies:
        copy.wait()
    square = (EXPERTS, EXPERTS)
    expert = lax.broadcasted_iota(jnp.int32, square, 0)
    lane = lax.broadcasted_iota(jnp.int32, square, 1)
    row = lax.broadcasted_iota(jnp.int32, (ROWS, EXPERTS), 0)
    spread = lax.broadcasted_iota(jnp.int32, (ROWS, EXPERTS), 1) % ROWS == row
    spread = jnp.where(spread, 1.0, 0.0).astype(BF16)
    ids = jnp.dot(ids_ref[...].astype(F32).astype(BF16), spread, preferred_element_type=F32)
    ids = ids.astype(jnp.int32)
    weights = jnp.dot(weights_ref[...], spread, preferred_element_type=F32)
    named = jnp.zeros(square, F32)
    value = jnp.zeros(square, F32)
    for k in range(8):
        hit = expert == ids[k : k + 1, :]
        named = jnp.where(hit, 1.0, named)
        value = jnp.where(hit, weights[k : k + 1, :], value)
    earlier = (expert // ROWS == lane // ROWS) & (expert < lane)
    before = jnp.dot(
        named.astype(BF16), jnp.where(earlier, 1.0, 0.0).astype(BF16), preferred_element_type=F32
    )
    lines = (EXPERTS * LINES, EXPERTS)
    line = lax.broadcasted_iota(jnp.int32, lines, 0)
    column = lax.broadcasted_iota(jnp.int32, lines, 1)
    same = (line // SLOTS) % CHUNKS == column // ROWS
    of_expert = line // LINES == column
    for out_ref, held in ((placing_ref, named), (mixing_ref, value)):
        table = jnp.zeros(lines, F32)
        for s in range(SLOTS):
            pick = jnp.where(of_expert & (line % SLOTS == s), 1.0, 0.0).astype(BF16)
            slot = jnp.where(before == s, held, 0.0).astype(BF16)
            table = table + jnp.dot(pick, slot, preferred_element_type=F32)
        out_ref[...] = jnp.where(same, table, 0.0).astype(BF16)
    for ref, out_ref in ((queries, qn), (other_ref, qn_other)):
        for h in range(QHEADS):
            head = ref[:, h * HD : (h + 1) * HD].astype(F32)
            out_ref[pl.ds(h * QROWS, QROWS), :] = rms_scale(head, gain[...]).astype(BF16)


def route(expert_ids, combine_weight, queries, q_gain, other):
    return pl.pallas_call(
        route_kernel,
        in_specs=[HBM()] * 4 + [VMEM()],
        out_specs=[VMEM()] * 4,
        out_shape=[jax.ShapeDtypeStruct((EXPERTS * LINES, EXPERTS), BF16)] * 2
        + [jax.ShapeDtypeStruct((QHEADS * QROWS, HD), BF16)] * 2,
        scratch_shapes=[
            pltpu.VMEM((8, ROWS), jnp.int32),
            pltpu.VMEM((8, ROWS), BF16),
            pltpu.VMEM((QROWS, QHEADS * HD), BF16),
            pltpu.VMEM((1, HD), F32),
            pltpu.SemaphoreType.DMA((4,)),
        ],
        compiler_params=params(16),
    )(expert_ids, combine_weight, queries, q_gain, other)


def dispatch_kernel(parts_ref, residual_ref, gain_ref, placing_ref, hidden_ref, out_ref, pieces):
    for n in range(8):
        columns = slice(n * 512, (n + 1) * 512)
        value = residual_ref[:, columns].astype(F32)
        for g in range(GROUPS):
            value = value + parts_ref[g, :, columns].astype(F32)
        hidden_ref[:, columns] = value
    normed = rms_scale(hidden_ref[...], gain_ref[...]).astype(BF16)
    for k in range(CHUNKS):
        pieces[pl.ds(k * ROWS, ROWS), :] = normed[:, k * PIECE : (k + 1) * PIECE]
    for g in range(8):
        lines = jnp.dot(
            placing_ref[pl.ds(g * GROUP_LINES, GROUP_LINES), :],
            pieces[...],
            preferred_element_type=F32,
        )
        out_ref[pl.ds(g * GROUP, GROUP)] = lines.astype(BF16).reshape(GROUP, LINES, PIECE)


def dispatch(parts, residual, norm_gain, placing):
    return pl.pallas_call(
        dispatch_kernel,
        in_specs=[VMEM()] * 4,
        out_specs=[VMEM()] * 2,
        out_shape=[
            jax.ShapeDtypeStruct((ROWS, WIDTH), F32),
            jax.ShapeDtypeStruct((EXPERTS, LINES, PIECE), BF16),
        ],
        scratch_shapes=[pltpu.VMEM((EXPERTS, PIECE), BF16)],
        compiler_params=params(12),
    )(parts, residual, norm_gain, placing)


def expert_kernel(
    lines_ref, up_ref, down_hbm, out_ref, rows, both, active, back, down_ref, sem
):
    copy = pltpu.make_async_copy(down_hbm, down_ref, sem)
    copy.start()
    size = (GROUP_LINES, GROUP_LINES)
    first = lax.broadcasted_iota(jnp.int32, size, 0)
    second = lax.broadcasted_iota(jnp.int32, size, 1)
    span = GROUP * SLOTS

    def held(by_chunk, by_source):
        source = (by_chunk % span) // SLOTS
        line = source * LINES + (by_chunk // span) * SLOTS + by_chunk % SLOTS
        return jnp.where(line == by_source, 1.0, 0.0).astype(BF16)

    gather, scatter = held(first, second), held(second, first)
    for g in range(8):
        group = lines_ref[pl.ds(g * GROUP, GROUP)].reshape(GROUP_LINES, PIECE)
        sorted_lines = jnp.dot(gather, group, preferred_element_type=F32).astype(BF16)
        for k in range(CHUNKS):
            rows[pl.ds(g * span, span), k * PIECE : (k + 1) * PIECE] = sorted_lines[
                k * span : (k + 1) * span, :
            ]
    for n in range(2 * FFE // 256):
        columns = slice(n * 256, (n + 1) * 256)
        both[:, columns] = jnp.dot(rows[...], up_ref[:, columns], preferred_element_type=F32)
    gate = both[:, :FFE]
    active[...] = (gate * jax.nn.sigmoid(gate) * both[:, FFE:]).astype(BF16)
    copy.wait()
    for k in range(CHUNKS):
        columns = slice(k * PIECE, (k + 1) * PIECE)
        down = jnp.dot(active[...], down_ref[:, columns], preferred_element_type=F32)
        down = down.astype(BF16)
        for g in range(8):
            back[g, pl.ds(k * span, span), :] = down[g * span : (g + 1) * span, :]
    for g in range(8):
        lines = jnp.dot(scatter, back[g], preferred_element_type=F32).astype(BF16)
        out_ref[pl.ds(g * GROUP, GROUP)] = lines.reshape(GROUP, LINES, PIECE)


def experts(lines, gate_up, down):
    return pl.pallas_call(
        expert_kernel,
        in_specs=[VMEM(), VMEM(), HBM()],
        out_specs=VMEM(),
        out_shape=jax.ShapeDtypeStruct((EXPERTS, LINES, PIECE), BF16),
        scratch_shapes=[
            pltpu.VMEM((EXPERTS * SLOTS, WIDTH), BF16),
            pltpu.VMEM((EXPERTS * SLOTS, 2 * FFE), F32),
            pltpu.VMEM((EXPERTS * SLOTS, FFE), BF16),
            pltpu.VMEM((8, GROUP_LINES, PIECE), BF16),
            pltpu.VMEM((FFE, WIDTH), BF16),
            pltpu.SemaphoreType.DMA,
        ],
        compiler_params=params(24),
    )(lines, gate_up, down)


def combine_kernel(lines_ref, mixing_ref, hidden_ref, out_ref):
    lines = lines_ref[...].reshape(EXPERTS * LINES, PIECE)
    mixed = lax.dot_general(
        mixing_ref[...], lines, (((0,), (0,)), ((), ())), preferred_element_type=F32
    )
    for k in range(CHUNKS):
        columns = slice(k * PIECE, (k + 1) * PIECE)
        value = hidden_ref[:, columns] + mixed[k * ROWS : (k + 1) * ROWS, :]
        out_ref[:, columns] = value.astype(BF16)


def combine(lines, mixing, hidden):
    return pl.pallas_call(
        combine_kernel,
        in_specs=[VMEM()] * 3,
        out_specs=VMEM(),
        out_shape=jax.ShapeDtypeStruct((ROWS, WIDTH), BF16),
        compiler_params=params(12),
    )(lines, mixing, hidden)


def per_device(
    queries,
    cache,
    new_kv,
    q_gain,
    k_gain,
    out_weight,
    residual,
    norm_gain,
    expert_ids,
    combine_weight,
    prefix_len,
    w_gate_up,
    w_down,
):
    z, y, x, c = (lax.axis_index(name).astype(jnp.int32) for name in ("z", "y", "x", "c"))
    place = jnp.stack([prefix_len[0], z, y, x, c])
    held = functools.partial(pltpu.with_memory_space_constraint, memory_space=pltpu.HBM)
    swap = functools.partial(lax.ppermute, axis_name="c", perm=[(0, 1), (1, 0)])
    other = swap(queries)
    left, right = shift(1), shift(3)
    own = prep(place, held(cache), held(new_kv), held(k_gain.reshape(1, HD)))
    first_left, second_right = lax.ppermute(own[0], "x", left), lax.ppermute(own[1], "x", right)
    second_left, first_right = lax.ppermute(own[1], "x", left), lax.ppermute(own[0], "x", right)
    placing, mixing, qn, qn_other = route(
        held(expert_ids.T), held(combine_weight.T), held(queries), held(q_gain.reshape(1, HD)), other
    )
    first_left, second_right, placing, mixing, qn, qn_other = lax.optimization_barrier(
        (first_left, second_right, placing, mixing, qn, qn_other)
    )
    first, second = lax.ppermute(first_left, "x", left), lax.ppermute(second_right, "x", right)
    *state, weight = attend_near(place, qn, qn_other, *own, held(out_weight))
    parts = (first_left, second_left, first_right, second_right)
    acc, total, acc_other, total_other = attend_middle(place, qn, qn_other, state, parts)
    far = attend_far(False, place, qn_other, acc_other, total_other, first, second)
    far, acc, total = lax.optimization_barrier((far, acc, total))
    mine = attend_far(True, place, qn, acc, total, first, second)
    parts = project(mine, swap(far), weight)
    parts = lax.all_to_all(parts, ("z", "y"), split_axis=0, concat_axis=0, tiled=True)
    hidden, lines = dispatch(parts, residual, norm_gain.reshape(1, WIDTH), placing)
    everyone = ("z", "y", "x", "c")
    lines = lax.all_to_all(lines, everyone, split_axis=0, concat_axis=0, tiled=True)
    lines = experts(lines, w_gate_up[0], w_down[0])
    lines = lax.all_to_all(lines, everyone, split_axis=0, concat_axis=0, tiled=True)
    return combine(lines, mixing, hidden)


def solution(mesh):
    fine = Mesh(mesh.devices.reshape(4, 4, 4, 2), ("z", "y", "x", "c"))
    head, tok = ("z", "y"), ("x", "c")
    placed = (
        P(tok, head),
        P(None, tok, None),
        P(None, tok, None),
        P(),
        P(),
        P(head, None),
        P(tok + head, None),
        P(),
        P(tok + head, None),
        P(tok + head, None),
        P(),
        P(head + tok, None, None),
        P(head + tok, None, None),
    )
    return jax.shard_map(
        per_device, mesh=fine, in_specs=placed, out_specs=P(tok + head, None), check_vma=False
    )
```

```python
import functools
import math

import jax
import jax.numpy as jnp
from jax import lax
from jax.experimental import pallas as pl
from jax.experimental.pallas import tpu as pltpu
from jax.sharding import Mesh
from jax.sharding import PartitionSpec as P

HEADS = 64
KV_HEADS = 4
HD = 128
WIDTH = 4096
ROWS = 16
QROWS = 256
QHEADS = 4
CACHE_ROWS = 512
SHARD = CACHE_ROWS + QROWS
PART = SHARD // 2
GROUPS = 16
EXPERTS = 128
SLOTS = 2
CHUNKS = 8
PIECE = WIDTH // CHUNKS
LINES = CHUNKS * SLOTS
FFE = 768
GROUP = 16
GROUP_LINES = GROUP * LINES
EPSILON = 1e-06
SCALE = math.log2(math.e) / math.sqrt(HD)
MB = 1 << 20

F32 = jnp.float32
BF16 = jnp.bfloat16

VMEM = functools.partial(pl.BlockSpec, memory_space=pltpu.VMEM)
SMEM = functools.partial(pl.BlockSpec, memory_space=pltpu.SMEM)
HBM = functools.partial(pl.BlockSpec, memory_space=pltpu.HBM)


def params(limit):
    return pltpu.CompilerParams(vmem_limit_bytes=limit * MB)


def rms_scale(values, gain):
    mean_square = jnp.mean(values * values, axis=-1, keepdims=True)
    return values * lax.rsqrt(mean_square + EPSILON) * gain


def shift(step):
    return [(i, (i + step) % 4) for i in range(4)]


def prep_kernel(place_ref, cache_ref, new_ref, gain_ref, first, second, cache, new, gain, sems):
    head = place_ref[1]
    copies = (
        pltpu.make_async_copy(gain_ref, gain, sems.at[0]),
        pltpu.make_async_copy(cache_ref.at[head], cache, sems.at[1]),
        pltpu.make_async_copy(new_ref.at[head], new, sems.at[2]),
    )
    for copy in copies:
        copy.start()
    for copy in copies:
        copy.wait()
    rest = CACHE_ROWS - PART
    for ref, start, out_ref, there, rows in (
        (cache, 0, first, 0, PART),
        (cache, PART, second, 0, rest),
        (new, 0, second, rest, QROWS),
    ):
        held = ref[pl.ds(start, rows), :]
        keys = rms_scale(held[:, :HD].astype(F32), gain[...]).astype(BF16)
        out_ref[pl.ds(there, rows), :HD] = keys
        out_ref[pl.ds(there, rows), HD:] = held[:, HD:]


def prep(place, cache, new_kv, k_gain):
    return pl.pallas_call(
        prep_kernel,
        in_specs=[SMEM(), HBM(), HBM(), HBM()],
        out_specs=[VMEM()] * 2,
        out_shape=[jax.ShapeDtypeStruct((PART, 2 * HD), BF16)] * 2,
        scratch_shapes=[
            pltpu.VMEM((CACHE_ROWS, 2 * HD), BF16),
            pltpu.VMEM((QROWS, 2 * HD), BF16),
            pltpu.VMEM((1, HD), F32),
            pltpu.SemaphoreType.DMA((3,)),
        ],
        compiler_params=params(8),
    )(place, cache, new_kv, k_gain)


def join(first, second, whole):
    whole[pl.ds(0, PART), :] = first[...]
    whole[pl.ds(PART, PART), :] = second[...]


def seen_blocks(limit, x, c, own, distances, shards, qn, acc, total):
    def block(ref, start, rows, mask=None):
        keys = ref[pl.ds(start, rows), :HD]
        values = ref[pl.ds(start, rows), HD:]
        scores = lax.dot_general(
            qn[...], keys, (((1,), (1,)), ((), ())), preferred_element_type=F32
        )
        weights = jnp.exp2(scores * SCALE)
        if mask is not None:
            weights = jnp.where(mask, weights, 0.0)
        part = weights[:, :HD]
        for i in range(1, rows // HD):
            part = part + weights[:, i * HD : (i + 1) * HD]
        total[...] += part
        acc[...] += jnp.dot(weights.astype(BF16), values, preferred_element_type=F32)

    tok = x * 2 + (c if own else 1 - c)
    for distance, ref in zip(distances, shards):
        owner = lax.rem(x + 4 - distance, 4) * 2 + c
        visible = limit - owner * CACHE_ROWS
        whole, earlier = visible >= CACHE_ROWS, owner < tok

        @pl.when(whole & earlier)
        def _():
            block(ref, 0, SHARD)

        @pl.when(whole & jnp.logical_not(earlier))
        def _():
            block(ref, 0, CACHE_ROWS)

        @pl.when((visible > 0) & (visible < CACHE_ROWS))
        def _():
            key = lax.broadcasted_iota(jnp.int32, (QHEADS * QROWS, CACHE_ROWS), 1)
            block(ref, 0, CACHE_ROWS, key < visible)

        @pl.when(jnp.logical_not(whole) & earlier)
        def _():
            block(ref, CACHE_ROWS, QROWS)

        if own and distance == 0:
            key = lax.broadcasted_iota(jnp.int32, (QHEADS * QROWS, QROWS), 1)
            query = lax.broadcasted_iota(jnp.int32, (QHEADS * QROWS, QROWS), 0)
            block(ref, CACHE_ROWS, QROWS, key <= lax.rem(query, QROWS))


STATE = jax.ShapeDtypeStruct((QHEADS * QROWS, HD), F32)
WHOLE = pltpu.VMEM((SHARD, 2 * HD), BF16)


def near_kernel(
    place_ref, qn, qn_other, first, second, weight_ref,
    acc, total, acc_other, total_other, weight, shard, sem,
):
    copy = pltpu.make_async_copy(weight_ref, weight, sem)
    copy.start()
    limit, x, c = place_ref[0], place_ref[3], place_ref[4]
    join(first, second, shard)
    for ref in (acc, total, acc_other, total_other):
        ref[...] = jnp.zeros_like(ref)
    seen_blocks(limit, x, c, False, (0,), (shard,), qn_other, acc_other, total_other)
    seen_blocks(limit, x, c, True, (0,), (shard,), qn, acc, total)
    copy.wait()


def attend_near(place, qn, qn_other, first, second, weight):
    return pl.pallas_call(
        near_kernel,
        in_specs=[SMEM()] + [VMEM()] * 4 + [HBM()],
        out_specs=[VMEM()] * 5,
        out_shape=[STATE] * 4 + [jax.ShapeDtypeStruct(weight.shape, BF16)],
        scratch_shapes=[WHOLE, pltpu.SemaphoreType.DMA],
        compiler_params=params(20),
    )(place, qn, qn_other, first, second, weight)


def middle_kernel(place_ref, qn, qn_other, *refs):
    before, parts, after, shards = refs[:4], refs[4:8], refs[8:12], refs[12:]
    limit, x, c = place_ref[0], place_ref[3], place_ref[4]
    for ref, out_ref in zip(before, after):
        out_ref[...] = ref[...]
    join(parts[0], parts[1], shards[0])
    join(parts[2], parts[3], shards[1])
    seen_blocks(limit, x, c, False, (1, 3), shards, qn_other, after[2], after[3])
    seen_blocks(limit, x, c, True, (1, 3), shards, qn, after[0], after[1])


def attend_middle(place, qn, qn_other, state, parts):
    return pl.pallas_call(
        middle_kernel,
        in_specs=[SMEM()] + [VMEM()] * 10,
        out_specs=[VMEM()] * 4,
        out_shape=[STATE] * 4,
        scratch_shapes=[WHOLE] * 2,
        compiler_params=params(16),
    )(place, qn, qn_other, *state, *parts)


def far_kernel(own, place_ref, qn, acc_ref, total_ref, first, second, out_ref, acc, total, shard):
    limit, x, c = place_ref[0], place_ref[3], place_ref[4]
    acc[...] = acc_ref[...]
    total[...] = total_ref[...]
    join(first, second, shard)
    seen_blocks(limit, x, c, own, (2,), (shard,), qn, acc, total)
    out_ref[:, :HD] = acc[...]
    out_ref[:, HD:] = total[...]


def attend_far(own, place, qn, acc, total, first, second):
    return pl.pallas_call(
        functools.partial(far_kernel, own),
        in_specs=[SMEM()] + [VMEM()] * 5,
        out_specs=VMEM(),
        out_shape=jax.ShapeDtypeStruct((QHEADS * QROWS, 2 * HD), F32),
        scratch_shapes=[
            pltpu.VMEM((QHEADS * QROWS, HD), F32),
            pltpu.VMEM((QHEADS * QROWS, HD), F32),
            WHOLE,
        ],
        compiler_params=params(16),
    )(place, qn, acc, total, first, second)


def project_kernel(place_ref, own_ref, other_ref, weight, *refs):
    outs, attn, ordered = refs[:4], refs[4], refs[5]
    z, y, c = place_ref[1], place_ref[2], place_ref[4]
    for h in range(QHEADS):
        at = pl.ds(h * QROWS, QROWS)
        both = own_ref[at, :] + other_ref[at, :]
        whole = jnp.sum(both[:, HD:], axis=1, keepdims=True)
        attn[:, h * HD : (h + 1) * HD] = (both[:, :HD] / whole).astype(BF16)
    for k in range(4):
        for i in range(4):
            over_y = i * 4 + lax.rem(y + k, 4)
            over_z = lax.rem(z + k, 4) * 4 + i
            group = jnp.where(c == 0, over_y, over_z)
            start = pl.multiple_of(group * ROWS, ROWS)
            ordered[pl.ds((k * 4 + i) * ROWS, ROWS), :] = attn[pl.ds(start, ROWS), :]
    for n in range(8):
        part = slice(n * 512, (n + 1) * 512)
        product = jnp.dot(ordered[...], weight[:, part], preferred_element_type=F32)
        product = product.astype(BF16).reshape(GROUPS, ROWS, 512)
        for k in range(4):
            outs[k][:, :, part] = product[k * 4 : (k + 1) * 4]


def project(place, own, other, weight):
    return pl.pallas_call(
        project_kernel,
        in_specs=[SMEM()] + [VMEM()] * 3,
        out_specs=[VMEM()] * 4,
        out_shape=[jax.ShapeDtypeStruct((4, ROWS, WIDTH), BF16)] * 4,
        scratch_shapes=[pltpu.VMEM((QROWS, QHEADS * HD), BF16)] * 2,
        compiler_params=params(16),
    )(place, own, other, weight)


def around(level, step):
    pairs = []
    for z in range(4):
        for y in range(4):
            for x in range(4):
                for c in range(2):
                    to_z, to_y = (z, (y + step) % 4) if c == level else ((z + step) % 4, y)
                    pairs.append((((z * 4 + y) * 4 + x) * 2 + c, ((to_z * 4 + to_y) * 4 + x) * 2 + c))
    return pairs


def sum_kernel(place_ref, *refs):
    parts, outs, held = refs[:4], refs[4:8], refs[8]
    mine = jnp.where(place_ref[4] == 0, place_ref[1], place_ref[2])
    for i in range(4):
        value = parts[0][i].astype(F32)
        for other in parts[1:]:
            value = value + other[i].astype(F32)
        held[i] = value.astype(BF16)
    for k in range(4):
        outs[k][...] = held[lax.rem(mine + k, 4)]


def first_sum(place, parts):
    return pl.pallas_call(
        sum_kernel,
        in_specs=[SMEM()] + [VMEM()] * 4,
        out_specs=[VMEM()] * 4,
        out_shape=[jax.ShapeDtypeStruct((ROWS, WIDTH), BF16)] * 4,
        scratch_shapes=[pltpu.VMEM((4, ROWS, WIDTH), BF16)],
        compiler_params=params(12),
    )(place, *parts)


def route_kernel(
    ids_hbm, weights_hbm, q_ref, gain_ref, other_ref, placing_ref, mixing_ref, qn, qn_other,
    ids_ref, weights_ref, queries, gain, sems,
):
    pairs = ((gain_ref, gain), (q_ref, queries), (ids_hbm, ids_ref), (weights_hbm, weights_ref))
    copies = [pltpu.make_async_copy(a, b, sems.at[i]) for i, (a, b) in enumerate(pairs)]
    for copy in copies:
        copy.start()
    for copy in copies:
        copy.wait()
    square = (EXPERTS, EXPERTS)
    expert = lax.broadcasted_iota(jnp.int32, square, 0)
    lane = lax.broadcasted_iota(jnp.int32, square, 1)
    row = lax.broadcasted_iota(jnp.int32, (ROWS, EXPERTS), 0)
    spread = lax.broadcasted_iota(jnp.int32, (ROWS, EXPERTS), 1) % ROWS == row
    spread = jnp.where(spread, 1.0, 0.0).astype(BF16)
    ids = jnp.dot(ids_ref[...].astype(F32).astype(BF16), spread, preferred_element_type=F32)
    ids = ids.astype(jnp.int32)
    weights = jnp.dot(weights_ref[...], spread, preferred_element_type=F32)
    named = jnp.zeros(square, F32)
    value = jnp.zeros(square, F32)
    for k in range(8):
        hit = expert == ids[k : k + 1, :]
        named = jnp.where(hit, 1.0, named)
        value = jnp.where(hit, weights[k : k + 1, :], value)
    earlier = (expert // ROWS == lane // ROWS) & (expert < lane)
    before = jnp.dot(
        named.astype(BF16), jnp.where(earlier, 1.0, 0.0).astype(BF16), preferred_element_type=F32
    )
    lines = (EXPERTS * LINES, EXPERTS)
    line = lax.broadcasted_iota(jnp.int32, lines, 0)
    column = lax.broadcasted_iota(jnp.int32, lines, 1)
    same = (line // SLOTS) % CHUNKS == column // ROWS
    of_expert = line // LINES == column
    for out_ref, held in ((placing_ref, named), (mixing_ref, value)):
        table = jnp.zeros(lines, F32)
        for s in range(SLOTS):
            pick = jnp.where(of_expert & (line % SLOTS == s), 1.0, 0.0).astype(BF16)
            slot = jnp.where(before == s, held, 0.0).astype(BF16)
            table = table + jnp.dot(pick, slot, preferred_element_type=F32)
        out_ref[...] = jnp.where(same, table, 0.0).astype(BF16)
    for ref, out_ref in ((queries, qn), (other_ref, qn_other)):
        for h in range(QHEADS):
            head = ref[:, h * HD : (h + 1) * HD].astype(F32)
            out_ref[pl.ds(h * QROWS, QROWS), :] = rms_scale(head, gain[...]).astype(BF16)


def route(expert_ids, combine_weight, queries, q_gain, other):
    return pl.pallas_call(
        route_kernel,
        in_specs=[HBM()] * 4 + [VMEM()],
        out_specs=[VMEM()] * 4,
        out_shape=[jax.ShapeDtypeStruct((EXPERTS * LINES, EXPERTS), BF16)] * 2
        + [jax.ShapeDtypeStruct((QHEADS * QROWS, HD), BF16)] * 2,
        scratch_shapes=[
            pltpu.VMEM((8, ROWS), jnp.int32),
            pltpu.VMEM((8, ROWS), BF16),
            pltpu.VMEM((QROWS, QHEADS * HD), BF16),
            pltpu.VMEM((1, HD), F32),
            pltpu.SemaphoreType.DMA((4,)),
        ],
        compiler_params=params(16),
    )(expert_ids, combine_weight, queries, q_gain, other)


def dispatch_kernel(*refs):
    parts, refs = refs[:4], refs[4:]
    residual_ref, gain_ref, placing_ref, hidden_ref, out_ref, pieces = refs
    for n in range(8):
        columns = slice(n * 512, (n + 1) * 512)
        value = residual_ref[:, columns].astype(F32)
        for part in parts:
            value = value + part[:, columns].astype(F32)
        hidden_ref[:, columns] = value
    normed = rms_scale(hidden_ref[...], gain_ref[...]).astype(BF16)
    for k in range(CHUNKS):
        pieces[pl.ds(k * ROWS, ROWS), :] = normed[:, k * PIECE : (k + 1) * PIECE]
    for g in range(8):
        lines = jnp.dot(
            placing_ref[pl.ds(g * GROUP_LINES, GROUP_LINES), :],
            pieces[...],
            preferred_element_type=F32,
        )
        out_ref[pl.ds(g * GROUP, GROUP)] = lines.astype(BF16).reshape(GROUP, LINES, PIECE)


def dispatch(parts, residual, norm_gain, placing):
    return pl.pallas_call(
        dispatch_kernel,
        in_specs=[VMEM()] * 7,
        out_specs=[VMEM()] * 2,
        out_shape=[
            jax.ShapeDtypeStruct((ROWS, WIDTH), F32),
            jax.ShapeDtypeStruct((EXPERTS, LINES, PIECE), BF16),
        ],
        scratch_shapes=[pltpu.VMEM((EXPERTS, PIECE), BF16)],
        compiler_params=params(12),
    )(*parts, residual, norm_gain, placing)


def expert_kernel(
    lines_ref, up_ref, down_hbm, out_ref, rows, both, active, back, down_ref, sem
):
    copy = pltpu.make_async_copy(down_hbm, down_ref, sem)
    copy.start()
    size = (GROUP_LINES, GROUP_LINES)
    first = lax.broadcasted_iota(jnp.int32, size, 0)
    second = lax.broadcasted_iota(jnp.int32, size, 1)
    span = GROUP * SLOTS

    def held(by_chunk, by_source):
        source = (by_chunk % span) // SLOTS
        line = source * LINES + (by_chunk // span) * SLOTS + by_chunk % SLOTS
        return jnp.where(line == by_source, 1.0, 0.0).astype(BF16)

    gather, scatter = held(first, second), held(second, first)
    for g in range(8):
        group = lines_ref[pl.ds(g * GROUP, GROUP)].reshape(GROUP_LINES, PIECE)
        sorted_lines = jnp.dot(gather, group, preferred_element_type=F32).astype(BF16)
        for k in range(CHUNKS):
            rows[pl.ds(g * span, span), k * PIECE : (k + 1) * PIECE] = sorted_lines[
                k * span : (k + 1) * span, :
            ]
    for n in range(2 * FFE // 256):
        columns = slice(n * 256, (n + 1) * 256)
        both[:, columns] = jnp.dot(rows[...], up_ref[:, columns], preferred_element_type=F32)
    gate = both[:, :FFE]
    active[...] = (gate * jax.nn.sigmoid(gate) * both[:, FFE:]).astype(BF16)
    copy.wait()
    for k in range(CHUNKS):
        columns = slice(k * PIECE, (k + 1) * PIECE)
        down = jnp.dot(active[...], down_ref[:, columns], preferred_element_type=F32)
        down = down.astype(BF16)
        for g in range(8):
            back[g, pl.ds(k * span, span), :] = down[g * span : (g + 1) * span, :]
    for g in range(8):
        lines = jnp.dot(scatter, back[g], preferred_element_type=F32).astype(BF16)
        out_ref[pl.ds(g * GROUP, GROUP)] = lines.reshape(GROUP, LINES, PIECE)


def experts(lines, gate_up, down):
    return pl.pallas_call(
        expert_kernel,
        in_specs=[VMEM(), VMEM(), HBM()],
        out_specs=VMEM(),
        out_shape=jax.ShapeDtypeStruct((EXPERTS, LINES, PIECE), BF16),
        scratch_shapes=[
            pltpu.VMEM((EXPERTS * SLOTS, WIDTH), BF16),
            pltpu.VMEM((EXPERTS * SLOTS, 2 * FFE), F32),
            pltpu.VMEM((EXPERTS * SLOTS, FFE), BF16),
            pltpu.VMEM((8, GROUP_LINES, PIECE), BF16),
            pltpu.VMEM((FFE, WIDTH), BF16),
            pltpu.SemaphoreType.DMA,
        ],
        compiler_params=params(24),
    )(lines, gate_up, down)


def combine_kernel(lines_ref, mixing_ref, hidden_ref, out_ref):
    lines = lines_ref[...].reshape(EXPERTS * LINES, PIECE)
    mixed = lax.dot_general(
        mixing_ref[...], lines, (((0,), (0,)), ((), ())), preferred_element_type=F32
    )
    for k in range(CHUNKS):
        columns = slice(k * PIECE, (k + 1) * PIECE)
        value = hidden_ref[:, columns] + mixed[k * ROWS : (k + 1) * ROWS, :]
        out_ref[:, columns] = value.astype(BF16)


def combine(lines, mixing, hidden):
    return pl.pallas_call(
        combine_kernel,
        in_specs=[VMEM()] * 3,
        out_specs=VMEM(),
        out_shape=jax.ShapeDtypeStruct((ROWS, WIDTH), BF16),
        compiler_params=params(12),
    )(lines, mixing, hidden)


def per_device(
    queries,
    cache,
    new_kv,
    q_gain,
    k_gain,
    out_weight,
    residual,
    norm_gain,
    expert_ids,
    combine_weight,
    prefix_len,
    w_gate_up,
    w_down,
):
    z, y, x, c = (lax.axis_index(name).astype(jnp.int32) for name in ("z", "y", "x", "c"))
    place = jnp.stack([prefix_len[0], z, y, x, c])
    held = functools.partial(pltpu.with_memory_space_constraint, memory_space=pltpu.HBM)
    swap = functools.partial(lax.ppermute, axis_name="c", perm=[(0, 1), (1, 0)])
    other = swap(queries)
    left, right = shift(1), shift(3)
    own = prep(place, held(cache), held(new_kv), held(k_gain.reshape(1, HD)))
    first_left, second_right = lax.ppermute(own[0], "x", left), lax.ppermute(own[1], "x", right)
    second_left, first_right = lax.ppermute(own[1], "x", left), lax.ppermute(own[0], "x", right)
    placing, mixing, qn, qn_other = route(
        held(expert_ids.T), held(combine_weight.T), held(queries), held(q_gain.reshape(1, HD)), other
    )
    first_left, second_right, placing, mixing, qn, qn_other = lax.optimization_barrier(
        (first_left, second_right, placing, mixing, qn, qn_other)
    )
    first, second = lax.ppermute(first_left, "x", left), lax.ppermute(second_right, "x", right)
    *state, weight = attend_near(place, qn, qn_other, *own, held(out_weight))
    parts = (first_left, second_left, first_right, second_right)
    acc, total, acc_other, total_other = attend_middle(place, qn, qn_other, state, parts)
    far = attend_far(False, place, qn_other, acc_other, total_other, first, second)
    far, acc, total = lax.optimization_barrier((far, acc, total))
    mine = attend_far(True, place, qn, acc, total, first, second)
    everyone = ("z", "y", "x", "c")
    parts = project(place, mine, swap(far), weight)
    for level in range(2):
        if level:
            parts = first_sum(place, parts)
        moved = [lax.ppermute(parts[k], everyone, around(level, k)) for k in (1, 2, 3)]
        parts = [parts[0], *moved]
    hidden, lines = dispatch(parts, residual, norm_gain.reshape(1, WIDTH), placing)
    lines = lax.all_to_all(lines, everyone, split_axis=0, concat_axis=0, tiled=True)
    lines = experts(lines, w_gate_up[0], w_down[0])
    lines = lax.all_to_all(lines, everyone, split_axis=0, concat_axis=0, tiled=True)
    return combine(lines, mixing, hidden)


def solution(mesh):
    fine = Mesh(mesh.devices.reshape(4, 4, 4, 2), ("z", "y", "x", "c"))
    head, tok = ("z", "y"), ("x", "c")
    placed = (
        P(tok, head),
        P(None, tok, None),
        P(None, tok, None),
        P(),
        P(),
        P(head, None),
        P(tok + head, None),
        P(),
        P(tok + head, None),
        P(tok + head, None),
        P(),
        P(head + tok, None, None),
        P(head + tok, None, None),
    )
    return jax.shard_map(
        per_device, mesh=fine, in_specs=placed, out_specs=P(tok + head, None), check_vma=False
    )
```

```python
import functools
import math

import jax
import jax.numpy as jnp
from jax import lax
from jax.experimental import pallas as pl
from jax.experimental.pallas import tpu as pltpu
from jax.sharding import Mesh
from jax.sharding import PartitionSpec as P

HEADS = 64
KV_HEADS = 4
HD = 128
WIDTH = 4096
ROWS = 16
QROWS = 256
QHEADS = 4
CACHE_ROWS = 512
SHARD = CACHE_ROWS + QROWS
PART = SHARD // 2
GROUPS = 16
EXPERTS = 128
SLOTS = 2
CHUNKS = 8
PIECE = WIDTH // CHUNKS
LINES = CHUNKS * SLOTS
FFE = 768
GROUP = 16
GROUP_LINES = GROUP * LINES
EPSILON = 1e-06
SCALE = math.log2(math.e) / math.sqrt(HD)
MB = 1 << 20

F32 = jnp.float32
BF16 = jnp.bfloat16

VMEM = functools.partial(pl.BlockSpec, memory_space=pltpu.VMEM)
SMEM = functools.partial(pl.BlockSpec, memory_space=pltpu.SMEM)
HBM = functools.partial(pl.BlockSpec, memory_space=pltpu.HBM)


def params(limit):
    return pltpu.CompilerParams(vmem_limit_bytes=limit * MB)


def rms_scale(values, gain):
    mean_square = jnp.mean(values * values, axis=-1, keepdims=True)
    return values * lax.rsqrt(mean_square + EPSILON) * gain


def shift(step):
    return [(i, (i + step) % 4) for i in range(4)]


def prep_kernel(place_ref, cache_ref, new_ref, gain_ref, first, second, cache, new, gain, sems):
    head = place_ref[1]
    copies = (
        pltpu.make_async_copy(gain_ref, gain, sems.at[0]),
        pltpu.make_async_copy(cache_ref.at[head], cache, sems.at[1]),
        pltpu.make_async_copy(new_ref.at[head], new, sems.at[2]),
    )
    for copy in copies:
        copy.start()
    for copy in copies:
        copy.wait()
    rest = CACHE_ROWS - PART
    for ref, start, out_ref, there, rows in (
        (cache, 0, first, 0, PART),
        (cache, PART, second, 0, rest),
        (new, 0, second, rest, QROWS),
    ):
        held = ref[pl.ds(start, rows), :]
        keys = rms_scale(held[:, :HD].astype(F32), gain[...]).astype(BF16)
        out_ref[pl.ds(there, rows), :HD] = keys
        out_ref[pl.ds(there, rows), HD:] = held[:, HD:]


def prep(place, cache, new_kv, k_gain):
    return pl.pallas_call(
        prep_kernel,
        in_specs=[SMEM(), HBM(), HBM(), HBM()],
        out_specs=[VMEM()] * 2,
        out_shape=[jax.ShapeDtypeStruct((PART, 2 * HD), BF16)] * 2,
        scratch_shapes=[
            pltpu.VMEM((CACHE_ROWS, 2 * HD), BF16),
            pltpu.VMEM((QROWS, 2 * HD), BF16),
            pltpu.VMEM((1, HD), F32),
            pltpu.SemaphoreType.DMA((3,)),
        ],
        compiler_params=params(8),
    )(place, cache, new_kv, k_gain)


def join(first, second, whole):
    whole[pl.ds(0, PART), :] = first[...]
    whole[pl.ds(PART, PART), :] = second[...]


def add_block(ref, start, rows, qn, acc, total, mask=None):
    keys = ref[pl.ds(start, rows), :HD]
    values = ref[pl.ds(start, rows), HD:]
    scores = lax.dot_general(qn[...], keys, (((1,), (1,)), ((), ())), preferred_element_type=F32)
    weights = jnp.exp2(scores * SCALE)
    if mask is not None:
        weights = jnp.where(mask, weights, 0.0)
    part = weights[:, :HD]
    for i in range(1, rows // HD):
        part = part + weights[:, i * HD : (i + 1) * HD]
    total[...] += part
    acc[...] += jnp.dot(weights.astype(BF16), values, preferred_element_type=F32)


def add_shard(place_ref, who, distance, ref, qn, acc, total):
    limit, x, c = place_ref[0], place_ref[3], place_ref[4]
    tok = x * 2 + lax.rem(c + who, 2)
    owner = lax.rem(x + 4 - distance, 4) * 2 + c
    visible = limit - owner * CACHE_ROWS
    whole, earlier = visible >= CACHE_ROWS, owner < tok

    @pl.when(whole & earlier)
    def _():
        add_block(ref, 0, SHARD, qn, acc, total)

    @pl.when(whole & jnp.logical_not(earlier))
    def _():
        add_block(ref, 0, CACHE_ROWS, qn, acc, total)

    @pl.when((visible > 0) & (visible < CACHE_ROWS))
    def _():
        key = lax.broadcasted_iota(jnp.int32, (QHEADS * QROWS, CACHE_ROWS), 1)
        add_block(ref, 0, CACHE_ROWS, qn, acc, total, key < visible)

    @pl.when(jnp.logical_not(whole) & earlier)
    def _():
        add_block(ref, CACHE_ROWS, QROWS, qn, acc, total)


STATE = jax.ShapeDtypeStruct((2, QHEADS * QROWS, HD), F32)


def near_kernel(place_ref, qn, first, second, weight_ref, acc, total, weight, shard, sem):
    copy = pltpu.make_async_copy(weight_ref, weight, sem)
    copy.start()
    join(first, second, shard)
    acc[...] = jnp.zeros_like(acc)
    total[...] = jnp.zeros_like(total)

    @pl.loop(0, 2)
    def _(who):
        add_shard(place_ref, who, 0, shard, qn.at[who], acc.at[who], total.at[who])

    key = lax.broadcasted_iota(jnp.int32, (QHEADS * QROWS, QROWS), 1)
    query = lax.broadcasted_iota(jnp.int32, (QHEADS * QROWS, QROWS), 0)
    mask = key <= lax.rem(query, QROWS)
    add_block(shard, CACHE_ROWS, QROWS, qn.at[0], acc.at[0], total.at[0], mask)
    copy.wait()


def attend_near(place, qn, first, second, weight):
    return pl.pallas_call(
        near_kernel,
        in_specs=[SMEM()] + [VMEM()] * 3 + [HBM()],
        out_specs=[VMEM()] * 3,
        out_shape=[STATE, STATE, jax.ShapeDtypeStruct(weight.shape, BF16)],
        scratch_shapes=[pltpu.VMEM((SHARD, 2 * HD), BF16), pltpu.SemaphoreType.DMA],
        compiler_params=params(20),
    )(place, qn, first, second, weight)


def middle_kernel(place_ref, qn, acc_ref, total_ref, *refs):
    parts, (acc, total, shards) = refs[:4], refs[4:]
    acc[...] = acc_ref[...]
    total[...] = total_ref[...]
    join(parts[0], parts[1], shards.at[0])
    join(parts[2], parts[3], shards.at[1])

    @pl.loop(0, 4)
    def _(step):
        who, side = lax.div(step, 2), lax.rem(step, 2)
        distance = 1 + 2 * side
        add_shard(
            place_ref, who, distance, shards.at[side], qn.at[who], acc.at[who], total.at[who]
        )


def attend_middle(place, qn, acc, total, parts):
    return pl.pallas_call(
        middle_kernel,
        in_specs=[SMEM()] + [VMEM()] * 7,
        out_specs=[VMEM()] * 2,
        out_shape=[STATE] * 2,
        scratch_shapes=[pltpu.VMEM((2, SHARD, 2 * HD), BF16)],
        compiler_params=params(16),
    )(place, qn, acc, total, *parts)


def far_kernel(who, place_ref, qn, acc_ref, total_ref, first, second, out_ref, acc, total, shard):
    acc[...] = acc_ref[who]
    total[...] = total_ref[who]
    join(first, second, shard)
    add_shard(place_ref, who, 2, shard, qn.at[who], acc, total)
    out_ref[:, :HD] = acc[...]
    out_ref[:, HD:] = total[...]


def attend_far(who, place, qn, acc, total, first, second):
    return pl.pallas_call(
        functools.partial(far_kernel, who),
        in_specs=[SMEM()] + [VMEM()] * 5,
        out_specs=VMEM(),
        out_shape=jax.ShapeDtypeStruct((QHEADS * QROWS, 2 * HD), F32),
        scratch_shapes=[
            pltpu.VMEM((QHEADS * QROWS, HD), F32),
            pltpu.VMEM((QHEADS * QROWS, HD), F32),
            pltpu.VMEM((SHARD, 2 * HD), BF16),
        ],
        compiler_params=params(16),
    )(place, qn, acc, total, first, second)


def project_kernel(place_ref, own_ref, other_ref, weight, *refs):
    outs, attn, ordered = refs[:4], refs[4], refs[5]
    z, y, c = place_ref[1], place_ref[2], place_ref[4]
    for h in range(QHEADS):
        at = pl.ds(h * QROWS, QROWS)
        both = own_ref[at, :] + other_ref[at, :]
        whole = jnp.sum(both[:, HD:], axis=1, keepdims=True)
        attn[:, h * HD : (h + 1) * HD] = (both[:, :HD] / whole).astype(BF16)
    for k in range(4):
        for i in range(4):
            over_y = i * 4 + lax.rem(y + k, 4)
            over_z = lax.rem(z + k, 4) * 4 + i
            group = jnp.where(c == 0, over_y, over_z)
            start = pl.multiple_of(group * ROWS, ROWS)
            ordered[pl.ds((k * 4 + i) * ROWS, ROWS), :] = attn[pl.ds(start, ROWS), :]
    for n in range(8):
        part = slice(n * 512, (n + 1) * 512)
        product = jnp.dot(ordered[...], weight[:, part], preferred_element_type=F32)
        product = product.astype(BF16).reshape(GROUPS, ROWS, 512)
        for k in range(4):
            outs[k][:, :, part] = product[k * 4 : (k + 1) * 4]


def project(place, own, other, weight):
    return pl.pallas_call(
        project_kernel,
        in_specs=[SMEM()] + [VMEM()] * 3,
        out_specs=[VMEM()] * 4,
        out_shape=[jax.ShapeDtypeStruct((4, ROWS, WIDTH), BF16)] * 4,
        scratch_shapes=[pltpu.VMEM((QROWS, QHEADS * HD), BF16)] * 2,
        compiler_params=params(16),
    )(place, own, other, weight)


def around(level, step):
    pairs = []
    for z in range(4):
        for y in range(4):
            for x in range(4):
                for c in range(2):
                    to_z, to_y = (z, (y + step) % 4) if c == level else ((z + step) % 4, y)
                    pairs.append((((z * 4 + y) * 4 + x) * 2 + c, ((to_z * 4 + to_y) * 4 + x) * 2 + c))
    return pairs


def sum_kernel(place_ref, *refs):
    parts, outs, held = refs[:4], refs[4:8], refs[8]
    mine = jnp.where(place_ref[4] == 0, place_ref[1], place_ref[2])
    for i in range(4):
        value = parts[0][i].astype(F32)
        for other in parts[1:]:
            value = value + other[i].astype(F32)
        held[i] = value.astype(BF16)
    for k in range(4):
        outs[k][...] = held[lax.rem(mine + k, 4)]


def first_sum(place, parts):
    return pl.pallas_call(
        sum_kernel,
        in_specs=[SMEM()] + [VMEM()] * 4,
        out_specs=[VMEM()] * 4,
        out_shape=[jax.ShapeDtypeStruct((ROWS, WIDTH), BF16)] * 4,
        scratch_shapes=[pltpu.VMEM((4, ROWS, WIDTH), BF16)],
        compiler_params=params(12),
    )(place, *parts)


def route_kernel(
    ids_hbm, weights_hbm, q_ref, gain_ref, other_ref, placing_ref, mixing_ref, qn,
    ids_ref, weights_ref, queries, gain, sems,
):
    pairs = ((gain_ref, gain), (q_ref, queries), (ids_hbm, ids_ref), (weights_hbm, weights_ref))
    copies = [pltpu.make_async_copy(a, b, sems.at[i]) for i, (a, b) in enumerate(pairs)]
    for copy in copies:
        copy.start()
    for copy in copies:
        copy.wait()
    square = (EXPERTS, EXPERTS)
    expert = lax.broadcasted_iota(jnp.int32, square, 0)
    lane = lax.broadcasted_iota(jnp.int32, square, 1)
    row = lax.broadcasted_iota(jnp.int32, (ROWS, EXPERTS), 0)
    spread = lax.broadcasted_iota(jnp.int32, (ROWS, EXPERTS), 1) % ROWS == row
    spread = jnp.where(spread, 1.0, 0.0).astype(BF16)
    ids = jnp.dot(ids_ref[...].astype(F32).astype(BF16), spread, preferred_element_type=F32)
    ids = ids.astype(jnp.int32)
    weights = jnp.dot(weights_ref[...], spread, preferred_element_type=F32)
    named = jnp.zeros(square, F32)
    value = jnp.zeros(square, F32)
    for k in range(8):
        hit = expert == ids[k : k + 1, :]
        named = jnp.where(hit, 1.0, named)
        value = jnp.where(hit, weights[k : k + 1, :], value)
    earlier = (expert // ROWS == lane // ROWS) & (expert < lane)
    before = jnp.dot(
        named.astype(BF16), jnp.where(earlier, 1.0, 0.0).astype(BF16), preferred_element_type=F32
    )
    lines = (EXPERTS * LINES, EXPERTS)
    line = lax.broadcasted_iota(jnp.int32, lines, 0)
    column = lax.broadcasted_iota(jnp.int32, lines, 1)
    same = (line // SLOTS) % CHUNKS == column // ROWS
    of_expert = line // LINES == column
    for out_ref, held in ((placing_ref, named), (mixing_ref, value)):
        table = jnp.zeros(lines, F32)
        for s in range(SLOTS):
            pick = jnp.where(of_expert & (line % SLOTS == s), 1.0, 0.0).astype(BF16)
            slot = jnp.where(before == s, held, 0.0).astype(BF16)
            table = table + jnp.dot(pick, slot, preferred_element_type=F32)
        out_ref[...] = jnp.where(same, table, 0.0).astype(BF16)
    for who, ref in enumerate((queries, other_ref)):
        for h in range(QHEADS):
            head = ref[:, h * HD : (h + 1) * HD].astype(F32)
            qn[who, pl.ds(h * QROWS, QROWS), :] = rms_scale(head, gain[...]).astype(BF16)


def route(expert_ids, combine_weight, queries, q_gain, other):
    return pl.pallas_call(
        route_kernel,
        in_specs=[HBM()] * 4 + [VMEM()],
        out_specs=[VMEM()] * 3,
        out_shape=[jax.ShapeDtypeStruct((EXPERTS * LINES, EXPERTS), BF16)] * 2
        + [jax.ShapeDtypeStruct((2, QHEADS * QROWS, HD), BF16)],
        scratch_shapes=[
            pltpu.VMEM((8, ROWS), jnp.int32),
            pltpu.VMEM((8, ROWS), BF16),
            pltpu.VMEM((QROWS, QHEADS * HD), BF16),
            pltpu.VMEM((1, HD), F32),
            pltpu.SemaphoreType.DMA((4,)),
        ],
        compiler_params=params(16),
    )(expert_ids, combine_weight, queries, q_gain, other)


def dispatch_kernel(*refs):
    parts, refs = refs[:4], refs[4:]
    residual_ref, gain_ref, placing_ref, hidden_ref, out_ref, pieces = refs
    for n in range(8):
        columns = slice(n * 512, (n + 1) * 512)
        value = residual_ref[:, columns].astype(F32)
        for part in parts:
            value = value + part[:, columns].astype(F32)
        hidden_ref[:, columns] = value
    normed = rms_scale(hidden_ref[...], gain_ref[...]).astype(BF16)
    for k in range(CHUNKS):
        pieces[pl.ds(k * ROWS, ROWS), :] = normed[:, k * PIECE : (k + 1) * PIECE]
    for g in range(8):
        lines = jnp.dot(
            placing_ref[pl.ds(g * GROUP_LINES, GROUP_LINES), :],
            pieces[...],
            preferred_element_type=F32,
        )
        out_ref[pl.ds(g * GROUP, GROUP)] = lines.astype(BF16).reshape(GROUP, LINES, PIECE)


def dispatch(parts, residual, norm_gain, placing):
    return pl.pallas_call(
        dispatch_kernel,
        in_specs=[VMEM()] * 7,
        out_specs=[VMEM()] * 2,
        out_shape=[
            jax.ShapeDtypeStruct((ROWS, WIDTH), F32),
            jax.ShapeDtypeStruct((EXPERTS, LINES, PIECE), BF16),
        ],
        scratch_shapes=[pltpu.VMEM((EXPERTS, PIECE), BF16)],
        compiler_params=params(12),
    )(*parts, residual, norm_gain, placing)


def expert_kernel(
    lines_ref, up_ref, down_hbm, out_ref, rows, both, active, back, down_ref, sem
):
    copy = pltpu.make_async_copy(down_hbm, down_ref, sem)
    copy.start()
    size = (GROUP_LINES, GROUP_LINES)
    first = lax.broadcasted_iota(jnp.int32, size, 0)
    second = lax.broadcasted_iota(jnp.int32, size, 1)
    span = GROUP * SLOTS

    def held(by_chunk, by_source):
        source = (by_chunk % span) // SLOTS
        line = source * LINES + (by_chunk // span) * SLOTS + by_chunk % SLOTS
        return jnp.where(line == by_source, 1.0, 0.0).astype(BF16)

    gather, scatter = held(first, second), held(second, first)
    for g in range(8):
        group = lines_ref[pl.ds(g * GROUP, GROUP)].reshape(GROUP_LINES, PIECE)
        sorted_lines = jnp.dot(gather, group, preferred_element_type=F32).astype(BF16)
        for k in range(CHUNKS):
            rows[pl.ds(g * span, span), k * PIECE : (k + 1) * PIECE] = sorted_lines[
                k * span : (k + 1) * span, :
            ]
    for n in range(2 * FFE // 256):
        columns = slice(n * 256, (n + 1) * 256)
        both[:, columns] = jnp.dot(rows[...], up_ref[:, columns], preferred_element_type=F32)
    gate = both[:, :FFE]
    active[...] = (gate * jax.nn.sigmoid(gate) * both[:, FFE:]).astype(BF16)
    copy.wait()
    for k in range(CHUNKS):
        columns = slice(k * PIECE, (k + 1) * PIECE)
        down = jnp.dot(active[...], down_ref[:, columns], preferred_element_type=F32)
        down = down.astype(BF16)
        for g in range(8):
            back[g, pl.ds(k * span, span), :] = down[g * span : (g + 1) * span, :]
    for g in range(8):
        lines = jnp.dot(scatter, back[g], preferred_element_type=F32).astype(BF16)
        out_ref[pl.ds(g * GROUP, GROUP)] = lines.reshape(GROUP, LINES, PIECE)


def experts(lines, gate_up, down):
    return pl.pallas_call(
        expert_kernel,
        in_specs=[VMEM(), VMEM(), HBM()],
        out_specs=VMEM(),
        out_shape=jax.ShapeDtypeStruct((EXPERTS, LINES, PIECE), BF16),
        scratch_shapes=[
            pltpu.VMEM((EXPERTS * SLOTS, WIDTH), BF16),
            pltpu.VMEM((EXPERTS * SLOTS, 2 * FFE), F32),
            pltpu.VMEM((EXPERTS * SLOTS, FFE), BF16),
            pltpu.VMEM((8, GROUP_LINES, PIECE), BF16),
            pltpu.VMEM((FFE, WIDTH), BF16),
            pltpu.SemaphoreType.DMA,
        ],
        compiler_params=params(24),
    )(lines, gate_up, down)


def combine_kernel(lines_ref, mixing_ref, hidden_ref, out_ref):
    lines = lines_ref[...].reshape(EXPERTS * LINES, PIECE)
    mixed = lax.dot_general(
        mixing_ref[...], lines, (((0,), (0,)), ((), ())), preferred_element_type=F32
    )
    for k in range(CHUNKS):
        columns = slice(k * PIECE, (k + 1) * PIECE)
        value = hidden_ref[:, columns] + mixed[k * ROWS : (k + 1) * ROWS, :]
        out_ref[:, columns] = value.astype(BF16)


def combine(lines, mixing, hidden):
    return pl.pallas_call(
        combine_kernel,
        in_specs=[VMEM()] * 3,
        out_specs=VMEM(),
        out_shape=jax.ShapeDtypeStruct((ROWS, WIDTH), BF16),
        compiler_params=params(12),
    )(lines, mixing, hidden)


def per_device(
    queries,
    cache,
    new_kv,
    q_gain,
    k_gain,
    out_weight,
    residual,
    norm_gain,
    expert_ids,
    combine_weight,
    prefix_len,
    w_gate_up,
    w_down,
):
    z, y, x, c = (lax.axis_index(name).astype(jnp.int32) for name in ("z", "y", "x", "c"))
    place = jnp.stack([prefix_len[0], z, y, x, c])
    held = functools.partial(pltpu.with_memory_space_constraint, memory_space=pltpu.HBM)
    swap = functools.partial(lax.ppermute, axis_name="c", perm=[(0, 1), (1, 0)])
    other = swap(queries)
    left, right = shift(1), shift(3)
    own = prep(place, held(cache), held(new_kv), held(k_gain.reshape(1, HD)))
    first_left, second_right = lax.ppermute(own[0], "x", left), lax.ppermute(own[1], "x", right)
    second_left, first_right = lax.ppermute(own[1], "x", left), lax.ppermute(own[0], "x", right)
    placing, mixing, qn = route(
        held(expert_ids.T), held(combine_weight.T), held(queries), held(q_gain.reshape(1, HD)), other
    )
    first_left, second_right, placing, mixing, qn = lax.optimization_barrier(
        (first_left, second_right, placing, mixing, qn)
    )
    first, second = lax.ppermute(first_left, "x", left), lax.ppermute(second_right, "x", right)
    acc, total, weight = attend_near(place, qn, *own, held(out_weight))
    parts = (first_left, second_left, first_right, second_right)
    acc, total = attend_middle(place, qn, acc, total, parts)
    far = attend_far(1, place, qn, acc, total, first, second)
    far, acc, total = lax.optimization_barrier((far, acc, total))
    mine = attend_far(0, place, qn, acc, total, first, second)
    everyone = ("z", "y", "x", "c")
    parts = project(place, mine, swap(far), weight)
    for level in range(2):
        if level:
            parts = first_sum(place, parts)
        moved = [lax.ppermute(parts[k], everyone, around(level, k)) for k in (1, 2, 3)]
        parts = [parts[0], *moved]
    hidden, lines = dispatch(parts, residual, norm_gain.reshape(1, WIDTH), placing)
    lines = lax.all_to_all(lines, everyone, split_axis=0, concat_axis=0, tiled=True)
    lines = experts(lines, w_gate_up[0], w_down[0])
    lines = lax.all_to_all(lines, everyone, split_axis=0, concat_axis=0, tiled=True)
    return combine(lines, mixing, hidden)


def solution(mesh):
    fine = Mesh(mesh.devices.reshape(4, 4, 4, 2), ("z", "y", "x", "c"))
    head, tok = ("z", "y"), ("x", "c")
    placed = (
        P(tok, head),
        P(None, tok, None),
        P(None, tok, None),
        P(),
        P(),
        P(head, None),
        P(tok + head, None),
        P(),
        P(tok + head, None),
        P(tok + head, None),
        P(),
        P(head + tok, None, None),
        P(head + tok, None, None),
    )
    return jax.shard_map(
        per_device, mesh=fine, in_specs=placed, out_specs=P(tok + head, None), check_vma=False
    )
```

```python
import functools
import math

import jax
import jax.numpy as jnp
from jax import lax
from jax.experimental import pallas as pl
from jax.experimental.pallas import tpu as pltpu
from jax.sharding import Mesh
from jax.sharding import PartitionSpec as P

HEADS = 64
KV_HEADS = 4
HD = 128
WIDTH = 4096
ROWS = 16
QROWS = 256
QHEADS = 4
CACHE_ROWS = 512
SHARD = CACHE_ROWS + QROWS
PART = SHARD // 2
GROUPS = 16
EXPERTS = 128
SLOTS = 2
CHUNKS = 8
PIECE = WIDTH // CHUNKS
LINES = CHUNKS * SLOTS
FFE = 768
GROUP = 16
GROUP_LINES = GROUP * LINES
EPSILON = 1e-06
SCALE = math.log2(math.e) / math.sqrt(HD)
MB = 1 << 20

F32 = jnp.float32
BF16 = jnp.bfloat16

VMEM = functools.partial(pl.BlockSpec, memory_space=pltpu.VMEM)
SMEM = functools.partial(pl.BlockSpec, memory_space=pltpu.SMEM)
HBM = functools.partial(pl.BlockSpec, memory_space=pltpu.HBM)


def params(limit):
    return pltpu.CompilerParams(vmem_limit_bytes=limit * MB)


def rms_scale(values, gain):
    mean_square = jnp.mean(values * values, axis=-1, keepdims=True)
    return values * lax.rsqrt(mean_square + EPSILON) * gain


def shift(step):
    return [(i, (i + step) % 4) for i in range(4)]


def prep_kernel(cache_ref, new_ref, gain_ref, first, second, cache, new, gain, sems):
    head = lax.axis_index("z")
    copies = (
        pltpu.make_async_copy(gain_ref, gain, sems.at[0]),
        pltpu.make_async_copy(cache_ref.at[head], cache, sems.at[1]),
        pltpu.make_async_copy(new_ref.at[head], new, sems.at[2]),
    )
    for copy in copies:
        copy.start()
    for copy in copies:
        copy.wait()
    rest = CACHE_ROWS - PART
    for ref, start, out_ref, there, rows in (
        (cache, 0, first, 0, PART),
        (cache, PART, second, 0, rest),
        (new, 0, second, rest, QROWS),
    ):
        held = ref[pl.ds(start, rows), :]
        keys = rms_scale(held[:, :HD].astype(F32), gain[...]).astype(BF16)
        out_ref[pl.ds(there, rows), :HD] = keys
        out_ref[pl.ds(there, rows), HD:] = held[:, HD:]


def prep(cache, new_kv, k_gain):
    return pl.pallas_call(
        prep_kernel,
        in_specs=[HBM()] * 3,
        out_specs=[VMEM()] * 2,
        out_shape=[jax.ShapeDtypeStruct((PART, 2 * HD), BF16)] * 2,
        scratch_shapes=[
            pltpu.VMEM((CACHE_ROWS, 2 * HD), BF16),
            pltpu.VMEM((QROWS, 2 * HD), BF16),
            pltpu.VMEM((1, HD), F32),
            pltpu.SemaphoreType.DMA((3,)),
        ],
        compiler_params=params(8),
    )(cache, new_kv, k_gain)


def join(first, second, whole):
    whole[pl.ds(0, PART), :] = first[...]
    whole[pl.ds(PART, PART), :] = second[...]


def add_block(ref, start, rows, qn, acc, total, mask=None):
    keys = ref[pl.ds(start, rows), :HD]
    values = ref[pl.ds(start, rows), HD:]
    scores = lax.dot_general(qn[...], keys, (((1,), (1,)), ((), ())), preferred_element_type=F32)
    weights = jnp.exp2(scores * SCALE)
    if mask is not None:
        weights = jnp.where(mask, weights, 0.0)
    part = weights[:, :HD]
    for i in range(1, rows // HD):
        part = part + weights[:, i * HD : (i + 1) * HD]
    total[...] += part
    acc[...] += jnp.dot(weights.astype(BF16), values, preferred_element_type=F32)


def add_shard(place_ref, who, distance, ref, qn, acc, total):
    limit, x, c = place_ref[0], place_ref[3], place_ref[4]
    tok = x * 2 + lax.rem(c + who, 2)
    owner = lax.rem(x + 4 - distance, 4) * 2 + c
    visible = limit - owner * CACHE_ROWS
    whole, earlier = visible >= CACHE_ROWS, owner < tok

    @pl.when(whole & earlier)
    def _():
        add_block(ref, 0, SHARD, qn, acc, total)

    @pl.when(whole & jnp.logical_not(earlier))
    def _():
        add_block(ref, 0, CACHE_ROWS, qn, acc, total)

    @pl.when((visible > 0) & (visible < CACHE_ROWS))
    def _():
        key = lax.broadcasted_iota(jnp.int32, (QHEADS * QROWS, CACHE_ROWS), 1)
        add_block(ref, 0, CACHE_ROWS, qn, acc, total, key < visible)

    @pl.when(jnp.logical_not(whole) & earlier)
    def _():
        add_block(ref, CACHE_ROWS, QROWS, qn, acc, total)


STATE = jax.ShapeDtypeStruct((2, QHEADS * QROWS, HD), F32)


def near_kernel(who, place_ref, qn, first, second, acc, total, shard):
    join(first, second, shard)
    acc[...] = jnp.zeros_like(acc)
    total[...] = jnp.zeros_like(total)
    add_shard(place_ref, who, 0, shard, qn.at[who], acc, total)
    if who == 0:
        key = lax.broadcasted_iota(jnp.int32, (QHEADS * QROWS, QROWS), 1)
        query = lax.broadcasted_iota(jnp.int32, (QHEADS * QROWS, QROWS), 0)
        mask = key <= lax.rem(query, QROWS)
        add_block(shard, CACHE_ROWS, QROWS, qn.at[0], acc, total, mask)


def attend_near(who, place, qn, first, second):
    return pl.pallas_call(
        functools.partial(near_kernel, who),
        in_specs=[SMEM()] + [VMEM()] * 3,
        out_specs=[VMEM()] * 2,
        out_shape=[jax.ShapeDtypeStruct((QHEADS * QROWS, HD), F32)] * 2,
        scratch_shapes=[pltpu.VMEM((SHARD, 2 * HD), BF16)],
        compiler_params=params(16),
    )(place, qn, first, second)


def middle_kernel(place_ref, qn, own_acc, own_total, other_acc, other_total, *refs):
    parts, (weight_ref, acc, total, weight, shards, sem) = refs[:4], refs[4:]
    copy = pltpu.make_async_copy(weight_ref, weight, sem)
    copy.start()
    acc[0], total[0] = own_acc[...], own_total[...]
    acc[1], total[1] = other_acc[...], other_total[...]
    join(parts[0], parts[1], shards.at[0])
    join(parts[2], parts[3], shards.at[1])

    @pl.loop(0, 4)
    def _(step):
        who, side = lax.div(step, 2), lax.rem(step, 2)
        distance = 1 + 2 * side
        add_shard(
            place_ref, who, distance, shards.at[side], qn.at[who], acc.at[who], total.at[who]
        )

    copy.wait()


def attend_middle(place, qn, own, other, parts, weight):
    return pl.pallas_call(
        middle_kernel,
        in_specs=[SMEM()] + [VMEM()] * 9 + [HBM()],
        out_specs=[VMEM()] * 3,
        out_shape=[STATE, STATE, jax.ShapeDtypeStruct(weight.shape, BF16)],
        scratch_shapes=[pltpu.VMEM((2, SHARD, 2 * HD), BF16), pltpu.SemaphoreType.DMA],
        compiler_params=params(20),
    )(place, qn, *own, *other, *parts, weight)


def far_kernel(who, place_ref, qn, acc_ref, total_ref, first, second, out_ref, acc, total, shard):
    acc[...] = acc_ref[who]
    total[...] = total_ref[who]
    join(first, second, shard)
    add_shard(place_ref, who, 2, shard, qn.at[who], acc, total)
    out_ref[:, :HD] = acc[...].astype(out_ref.dtype)
    out_ref[:, HD:] = total[...].astype(out_ref.dtype)


def attend_far(who, place, qn, acc, total, first, second):
    return pl.pallas_call(
        functools.partial(far_kernel, who),
        in_specs=[SMEM()] + [VMEM()] * 5,
        out_specs=VMEM(),
        out_shape=jax.ShapeDtypeStruct((QHEADS * QROWS, 2 * HD), BF16 if who else F32),
        scratch_shapes=[
            pltpu.VMEM((QHEADS * QROWS, HD), F32),
            pltpu.VMEM((QHEADS * QROWS, HD), F32),
            pltpu.VMEM((SHARD, 2 * HD), BF16),
        ],
        compiler_params=params(16),
    )(place, qn, acc, total, first, second)


def project_kernel(place_ref, own_ref, other_ref, weight, *refs):
    outs, attn, ordered = refs[:4], refs[4], refs[5]
    z, y, c = place_ref[1], place_ref[2], place_ref[4]
    for h in range(QHEADS):
        at = pl.ds(h * QROWS, QROWS)
        both = own_ref[at, :] + other_ref[at, :].astype(F32)
        whole = jnp.sum(both[:, HD:], axis=1, keepdims=True)
        attn[:, h * HD : (h + 1) * HD] = (both[:, :HD] / whole).astype(BF16)
    for k in range(4):
        for i in range(4):
            over_y = i * 4 + lax.rem(y + k, 4)
            over_z = lax.rem(z + k, 4) * 4 + i
            group = jnp.where(c == 0, over_y, over_z)
            start = pl.multiple_of(group * ROWS, ROWS)
            ordered[pl.ds((k * 4 + i) * ROWS, ROWS), :] = attn[pl.ds(start, ROWS), :]
    for n in range(8):
        part = slice(n * 512, (n + 1) * 512)
        product = jnp.dot(ordered[...], weight[:, part], preferred_element_type=F32)
        product = product.astype(BF16).reshape(GROUPS, ROWS, 512)
        for k in range(4):
            outs[k][:, :, part] = product[k * 4 : (k + 1) * 4]


def project(place, own, other, weight):
    return pl.pallas_call(
        project_kernel,
        in_specs=[SMEM()] + [VMEM()] * 3,
        out_specs=[VMEM()] * 4,
        out_shape=[jax.ShapeDtypeStruct((4, ROWS, WIDTH), BF16)] * 4,
        scratch_shapes=[pltpu.VMEM((QROWS, QHEADS * HD), BF16)] * 2,
        compiler_params=params(16),
    )(place, own, other, weight)


def around(level, step):
    pairs = []
    for z in range(4):
        for y in range(4):
            for x in range(4):
                for c in range(2):
                    to_z, to_y = (z, (y + step) % 4) if c == level else ((z + step) % 4, y)
                    pairs.append((((z * 4 + y) * 4 + x) * 2 + c, ((to_z * 4 + to_y) * 4 + x) * 2 + c))
    return pairs


def sum_kernel(place_ref, *refs):
    parts, outs, held = refs[:4], refs[4:8], refs[8]
    mine = jnp.where(place_ref[4] == 0, place_ref[1], place_ref[2])
    for i in range(4):
        value = parts[0][i].astype(F32)
        for other in parts[1:]:
            value = value + other[i].astype(F32)
        held[i] = value.astype(BF16)
    for k in range(4):
        outs[k][...] = held[lax.rem(mine + k, 4)]


def first_sum(place, parts):
    return pl.pallas_call(
        sum_kernel,
        in_specs=[SMEM()] + [VMEM()] * 4,
        out_specs=[VMEM()] * 4,
        out_shape=[jax.ShapeDtypeStruct((ROWS, WIDTH), BF16)] * 4,
        scratch_shapes=[pltpu.VMEM((4, ROWS, WIDTH), BF16)],
        compiler_params=params(12),
    )(place, *parts)


def route_kernel(
    ids_hbm, weights_hbm, q_ref, gain_ref, other_ref, placing_ref, mixing_ref, qn,
    ids_ref, weights_ref, queries, gain, sems,
):
    pairs = ((gain_ref, gain), (q_ref, queries), (ids_hbm, ids_ref), (weights_hbm, weights_ref))
    copies = [pltpu.make_async_copy(a, b, sems.at[i]) for i, (a, b) in enumerate(pairs)]
    for copy in copies:
        copy.start()
    for copy in copies:
        copy.wait()
    square = (EXPERTS, EXPERTS)
    expert = lax.broadcasted_iota(jnp.int32, square, 0)
    lane = lax.broadcasted_iota(jnp.int32, square, 1)
    row = lax.broadcasted_iota(jnp.int32, (ROWS, EXPERTS), 0)
    spread = lax.broadcasted_iota(jnp.int32, (ROWS, EXPERTS), 1) % ROWS == row
    spread = jnp.where(spread, 1.0, 0.0).astype(BF16)
    ids = jnp.dot(ids_ref[...].astype(F32).astype(BF16), spread, preferred_element_type=F32)
    ids = ids.astype(jnp.int32)
    weights = jnp.dot(weights_ref[...], spread, preferred_element_type=F32)
    named = jnp.zeros(square, F32)
    value = jnp.zeros(square, F32)
    for k in range(8):
        hit = expert == ids[k : k + 1, :]
        named = jnp.where(hit, 1.0, named)
        value = jnp.where(hit, weights[k : k + 1, :], value)
    earlier = (expert // ROWS == lane // ROWS) & (expert < lane)
    before = jnp.dot(
        named.astype(BF16), jnp.where(earlier, 1.0, 0.0).astype(BF16), preferred_element_type=F32
    )
    lines = (EXPERTS * LINES, EXPERTS)
    line = lax.broadcasted_iota(jnp.int32, lines, 0)
    column = lax.broadcasted_iota(jnp.int32, lines, 1)
    same = (line // SLOTS) % CHUNKS == column // ROWS
    of_expert = line // LINES == column
    for out_ref, held in ((placing_ref, named), (mixing_ref, value)):
        table = jnp.zeros(lines, F32)
        for s in range(SLOTS):
            pick = jnp.where(of_expert & (line % SLOTS == s), 1.0, 0.0).astype(BF16)
            slot = jnp.where(before == s, held, 0.0).astype(BF16)
            table = table + jnp.dot(pick, slot, preferred_element_type=F32)
        out_ref[...] = jnp.where(same, table, 0.0).astype(BF16)
    for who, ref in enumerate((queries, other_ref)):
        for h in range(QHEADS):
            head = ref[:, h * HD : (h + 1) * HD].astype(F32)
            qn[who, pl.ds(h * QROWS, QROWS), :] = rms_scale(head, gain[...]).astype(BF16)


def route(expert_ids, combine_weight, queries, q_gain, other):
    return pl.pallas_call(
        route_kernel,
        in_specs=[HBM()] * 4 + [VMEM()],
        out_specs=[VMEM()] * 3,
        out_shape=[jax.ShapeDtypeStruct((EXPERTS * LINES, EXPERTS), BF16)] * 2
        + [jax.ShapeDtypeStruct((2, QHEADS * QROWS, HD), BF16)],
        scratch_shapes=[
            pltpu.VMEM((8, ROWS), jnp.int32),
            pltpu.VMEM((8, ROWS), BF16),
            pltpu.VMEM((QROWS, QHEADS * HD), BF16),
            pltpu.VMEM((1, HD), F32),
            pltpu.SemaphoreType.DMA((4,)),
        ],
        compiler_params=params(16),
    )(expert_ids, combine_weight, queries, q_gain, other)


def dispatch_kernel(*refs):
    parts, refs = refs[:4], refs[4:]
    residual_ref, gain_ref, placing_ref, hidden_ref, out_ref, pieces = refs
    for n in range(8):
        columns = slice(n * 512, (n + 1) * 512)
        value = residual_ref[:, columns].astype(F32)
        for part in parts:
            value = value + part[:, columns].astype(F32)
        hidden_ref[:, columns] = value
    normed = rms_scale(hidden_ref[...], gain_ref[...]).astype(BF16)
    for k in range(CHUNKS):
        pieces[pl.ds(k * ROWS, ROWS), :] = normed[:, k * PIECE : (k + 1) * PIECE]
    for g in range(8):
        lines = jnp.dot(
            placing_ref[pl.ds(g * GROUP_LINES, GROUP_LINES), :],
            pieces[...],
            preferred_element_type=F32,
        )
        out_ref[pl.ds(g * GROUP, GROUP)] = lines.astype(BF16).reshape(GROUP, LINES, PIECE)


def dispatch(parts, residual, norm_gain, placing):
    return pl.pallas_call(
        dispatch_kernel,
        in_specs=[VMEM()] * 7,
        out_specs=[VMEM()] * 2,
        out_shape=[
            jax.ShapeDtypeStruct((ROWS, WIDTH), F32),
            jax.ShapeDtypeStruct((EXPERTS, LINES, PIECE), BF16),
        ],
        scratch_shapes=[pltpu.VMEM((EXPERTS, PIECE), BF16)],
        compiler_params=params(12),
    )(*parts, residual, norm_gain, placing)


def expert_kernel(
    lines_ref, up_ref, down_ref, out_ref, rows, both, active, back
):
    size = (GROUP_LINES, GROUP_LINES)
    first = lax.broadcasted_iota(jnp.int32, size, 0)
    second = lax.broadcasted_iota(jnp.int32, size, 1)
    span = GROUP * SLOTS

    def held(by_chunk, by_source):
        source = (by_chunk % span) // SLOTS
        line = source * LINES + (by_chunk // span) * SLOTS + by_chunk % SLOTS
        return jnp.where(line == by_source, 1.0, 0.0).astype(BF16)

    gather, scatter = held(first, second), held(second, first)
    for g in range(8):
        group = lines_ref[pl.ds(g * GROUP, GROUP)].reshape(GROUP_LINES, PIECE)
        sorted_lines = jnp.dot(gather, group, preferred_element_type=F32).astype(BF16)
        for k in range(CHUNKS):
            rows[pl.ds(g * span, span), k * PIECE : (k + 1) * PIECE] = sorted_lines[
                k * span : (k + 1) * span, :
            ]
    for n in range(2 * FFE // 256):
        columns = slice(n * 256, (n + 1) * 256)
        both[:, columns] = jnp.dot(rows[...], up_ref[:, columns], preferred_element_type=F32)
    gate = both[:, :FFE]
    active[...] = (gate * jax.nn.sigmoid(gate) * both[:, FFE:]).astype(BF16)
    for k in range(CHUNKS):
        columns = slice(k * PIECE, (k + 1) * PIECE)
        down = jnp.dot(active[...], down_ref[:, columns], preferred_element_type=F32)
        down = down.astype(BF16)
        for g in range(8):
            back[g, pl.ds(k * span, span), :] = down[g * span : (g + 1) * span, :]
    for g in range(8):
        lines = jnp.dot(scatter, back[g], preferred_element_type=F32).astype(BF16)
        out_ref[pl.ds(g * GROUP, GROUP)] = lines.reshape(GROUP, LINES, PIECE)


def experts(lines, gate_up, down):
    return pl.pallas_call(
        expert_kernel,
        in_specs=[VMEM()] * 3,
        out_specs=VMEM(),
        out_shape=jax.ShapeDtypeStruct((EXPERTS, LINES, PIECE), BF16),
        scratch_shapes=[
            pltpu.VMEM((EXPERTS * SLOTS, WIDTH), BF16),
            pltpu.VMEM((EXPERTS * SLOTS, 2 * FFE), F32),
            pltpu.VMEM((EXPERTS * SLOTS, FFE), BF16),
            pltpu.VMEM((8, GROUP_LINES, PIECE), BF16),
        ],
        compiler_params=params(18),
    )(lines, gate_up, down)


def combine_kernel(lines_ref, mixing_ref, hidden_ref, out_ref):
    lines = lines_ref[...].reshape(EXPERTS * LINES, PIECE)
    mixed = lax.dot_general(
        mixing_ref[...], lines, (((0,), (0,)), ((), ())), preferred_element_type=F32
    )
    for k in range(CHUNKS):
        columns = slice(k * PIECE, (k + 1) * PIECE)
        value = hidden_ref[:, columns] + mixed[k * ROWS : (k + 1) * ROWS, :]
        out_ref[:, columns] = value.astype(BF16)


def combine(lines, mixing, hidden):
    return pl.pallas_call(
        combine_kernel,
        in_specs=[VMEM()] * 3,
        out_specs=VMEM(),
        out_shape=jax.ShapeDtypeStruct((ROWS, WIDTH), BF16),
        compiler_params=params(12),
    )(lines, mixing, hidden)


def per_device(
    queries,
    cache,
    new_kv,
    q_gain,
    k_gain,
    out_weight,
    residual,
    norm_gain,
    expert_ids,
    combine_weight,
    prefix_len,
    w_gate_up,
    w_down,
):
    z, y, x, c = (lax.axis_index(name).astype(jnp.int32) for name in ("z", "y", "x", "c"))
    place = jnp.stack([prefix_len[0], z, y, x, c])
    held = functools.partial(pltpu.with_memory_space_constraint, memory_space=pltpu.HBM)
    swap = functools.partial(lax.ppermute, axis_name="c", perm=[(0, 1), (1, 0)])
    other = swap(queries)
    left, right = shift(1), shift(3)
    own = prep(held(cache), held(new_kv), held(k_gain.reshape(1, HD)))
    first_left, second_right = lax.ppermute(own[0], "x", left), lax.ppermute(own[1], "x", right)
    second_left, first_right = lax.ppermute(own[1], "x", left), lax.ppermute(own[0], "x", right)
    placing, mixing, qn = route(
        held(expert_ids.T), held(combine_weight.T), held(queries), held(q_gain.reshape(1, HD)), other
    )
    other = attend_near(1, place, qn, *own)
    first_left, second_right, placing, mixing, qn, *other = lax.optimization_barrier(
        (first_left, second_right, placing, mixing, qn, *other)
    )
    first, second = lax.ppermute(first_left, "x", left), lax.ppermute(second_right, "x", right)
    mine = attend_near(0, place, qn, *own)
    parts = (first_left, second_left, first_right, second_right)
    acc, total, weight = attend_middle(place, qn, mine, other, parts, held(out_weight))
    far = attend_far(1, place, qn, acc, total, first, second)
    far, acc, total = lax.optimization_barrier((far, acc, total))
    mine = attend_far(0, place, qn, acc, total, first, second)
    everyone = ("z", "y", "x", "c")
    parts = project(place, mine, swap(far), weight)
    for level in range(2):
        if level:
            parts = first_sum(place, parts)
        moved = [lax.ppermute(parts[k], everyone, around(level, k)) for k in (1, 2, 3)]
        parts = [parts[0], *moved]
    hidden, lines = dispatch(parts, residual, norm_gain.reshape(1, WIDTH), placing)
    lines = lax.all_to_all(lines, everyone, split_axis=0, concat_axis=0, tiled=True)
    lines = experts(lines, w_gate_up[0], w_down[0])
    lines = lax.all_to_all(lines, everyone, split_axis=0, concat_axis=0, tiled=True)
    return combine(lines, mixing, hidden)


def solution(mesh):
    fine = Mesh(mesh.devices.reshape(4, 4, 4, 2), ("z", "y", "x", "c"))
    head, tok = ("z", "y"), ("x", "c")
    placed = (
        P(tok, head),
        P(None, tok, None),
        P(None, tok, None),
        P(),
        P(),
        P(head, None),
        P(tok + head, None),
        P(),
        P(tok + head, None),
        P(tok + head, None),
        P(),
        P(head + tok, None, None),
        P(head + tok, None, None),
    )
    return jax.shard_map(
        per_device, mesh=fine, in_specs=placed, out_specs=P(tok + head, None), check_vma=False
    )
```

```python
import functools
import math

import jax
import jax.numpy as jnp
from jax import lax
from jax.experimental import pallas as pl
from jax.experimental.pallas import tpu as pltpu
from jax.sharding import Mesh
from jax.sharding import PartitionSpec as P

HEADS = 64
KV_HEADS = 4
HD = 128
WIDTH = 4096
ROWS = 16
QROWS = 256
QHEADS = 4
CACHE_ROWS = 512
SHARD = CACHE_ROWS + QROWS
PART = SHARD // 2
GROUPS = 16
EXPERTS = 128
SLOTS = 2
CHUNKS = 8
PIECE = WIDTH // CHUNKS
LINES = CHUNKS * SLOTS
FFE = 768
GROUP = 16
GROUP_LINES = GROUP * LINES
EPSILON = 1e-06
SCALE = math.log2(math.e) / math.sqrt(HD)
MB = 1 << 20

F32 = jnp.float32
BF16 = jnp.bfloat16

VMEM = functools.partial(pl.BlockSpec, memory_space=pltpu.VMEM)
SMEM = functools.partial(pl.BlockSpec, memory_space=pltpu.SMEM)
HBM = functools.partial(pl.BlockSpec, memory_space=pltpu.HBM)


def params(limit):
    return pltpu.CompilerParams(vmem_limit_bytes=limit * MB)


def rms_scale(values, gain):
    mean_square = jnp.mean(values * values, axis=-1, keepdims=True)
    return values * lax.rsqrt(mean_square + EPSILON) * gain


def shift(step):
    return [(i, (i + step) % 4) for i in range(4)]


def prep_kernel(cache_ref, new_ref, gain_ref, first, second, cache, new, gain, sems):
    head = lax.axis_index("z")
    copies = (
        pltpu.make_async_copy(gain_ref, gain, sems.at[0]),
        pltpu.make_async_copy(cache_ref.at[head], cache, sems.at[1]),
        pltpu.make_async_copy(new_ref.at[head], new, sems.at[2]),
    )
    for copy in copies:
        copy.start()
    for copy in copies:
        copy.wait()
    rest = CACHE_ROWS - PART
    for ref, start, out_ref, there, rows in (
        (cache, 0, first, 0, PART),
        (cache, PART, second, 0, rest),
        (new, 0, second, rest, QROWS),
    ):
        held = ref[pl.ds(start, rows), :]
        keys = rms_scale(held[:, :HD].astype(F32), gain[...]).astype(BF16)
        out_ref[pl.ds(there, rows), :HD] = keys
        out_ref[pl.ds(there, rows), HD:] = held[:, HD:]


def prep(cache, new_kv, k_gain):
    return pl.pallas_call(
        prep_kernel,
        in_specs=[HBM()] * 3,
        out_specs=[VMEM()] * 2,
        out_shape=[jax.ShapeDtypeStruct((PART, 2 * HD), BF16)] * 2,
        scratch_shapes=[
            pltpu.VMEM((CACHE_ROWS, 2 * HD), BF16),
            pltpu.VMEM((QROWS, 2 * HD), BF16),
            pltpu.VMEM((1, HD), F32),
            pltpu.SemaphoreType.DMA((3,)),
        ],
        compiler_params=params(8),
    )(cache, new_kv, k_gain)


def join(first, second, whole):
    whole[pl.ds(0, PART), :] = first[...]
    whole[pl.ds(PART, PART), :] = second[...]


def add_block(ref, start, rows, qn, acc, total, mask=None):
    keys = ref[pl.ds(start, rows), :HD]
    values = ref[pl.ds(start, rows), HD:]
    scores = lax.dot_general(qn[...], keys, (((1,), (1,)), ((), ())), preferred_element_type=F32)
    weights = jnp.exp2(scores * SCALE)
    if mask is not None:
        weights = jnp.where(mask, weights, 0.0)
    part = weights[:, :HD]
    for i in range(1, rows // HD):
        part = part + weights[:, i * HD : (i + 1) * HD]
    total[...] += part
    acc[...] += jnp.dot(weights.astype(BF16), values, preferred_element_type=F32)


def add_shard(place_ref, who, distance, ref, qn, acc, total):
    limit, x, c = place_ref[0], place_ref[3], place_ref[4]
    tok = x * 2 + lax.rem(c + who, 2)
    owner = lax.rem(x + 4 - distance, 4) * 2 + c
    visible = limit - owner * CACHE_ROWS
    whole, earlier = visible >= CACHE_ROWS, owner < tok

    @pl.when(whole & earlier)
    def _():
        add_block(ref, 0, SHARD, qn, acc, total)

    @pl.when(whole & jnp.logical_not(earlier))
    def _():
        add_block(ref, 0, CACHE_ROWS, qn, acc, total)

    @pl.when((visible > 0) & (visible < CACHE_ROWS))
    def _():
        key = lax.broadcasted_iota(jnp.int32, (QHEADS * QROWS, CACHE_ROWS), 1)
        add_block(ref, 0, CACHE_ROWS, qn, acc, total, key < visible)

    @pl.when(jnp.logical_not(whole) & earlier)
    def _():
        add_block(ref, CACHE_ROWS, QROWS, qn, acc, total)


STATE = jax.ShapeDtypeStruct((2, QHEADS * QROWS, HD), F32)


def near_kernel(who, place_ref, qn, first, second, acc, total, shard):
    join(first, second, shard)
    acc[...] = jnp.zeros_like(acc)
    total[...] = jnp.zeros_like(total)
    add_shard(place_ref, who, 0, shard, qn.at[who], acc, total)
    if who == 0:
        key = lax.broadcasted_iota(jnp.int32, (QHEADS * QROWS, QROWS), 1)
        query = lax.broadcasted_iota(jnp.int32, (QHEADS * QROWS, QROWS), 0)
        mask = key <= lax.rem(query, QROWS)
        add_block(shard, CACHE_ROWS, QROWS, qn.at[0], acc, total, mask)


def attend_near(who, place, qn, first, second):
    return pl.pallas_call(
        functools.partial(near_kernel, who),
        in_specs=[SMEM()] + [VMEM()] * 3,
        out_specs=[VMEM()] * 2,
        out_shape=[jax.ShapeDtypeStruct((QHEADS * QROWS, HD), F32)] * 2,
        scratch_shapes=[pltpu.VMEM((SHARD, 2 * HD), BF16)],
        compiler_params=params(16),
    )(place, qn, first, second)


def middle_kernel(place_ref, qn, own_acc, own_total, other_acc, other_total, *refs):
    parts, (weight_ref, acc, total, weight, shards, sem) = refs[:4], refs[4:]
    copy = pltpu.make_async_copy(weight_ref, weight, sem)
    copy.start()
    acc[0], total[0] = own_acc[...], own_total[...]
    acc[1], total[1] = other_acc[...], other_total[...]
    join(parts[0], parts[1], shards.at[0])
    join(parts[2], parts[3], shards.at[1])

    @pl.loop(0, 4)
    def _(step):
        who, side = lax.div(step, 2), lax.rem(step, 2)
        distance = 1 + 2 * side
        add_shard(
            place_ref, who, distance, shards.at[side], qn.at[who], acc.at[who], total.at[who]
        )

    copy.wait()


def attend_middle(place, qn, own, other, parts, weight):
    return pl.pallas_call(
        middle_kernel,
        in_specs=[SMEM()] + [VMEM()] * 9 + [HBM()],
        out_specs=[VMEM()] * 3,
        out_shape=[STATE, STATE, jax.ShapeDtypeStruct(weight.shape, BF16)],
        scratch_shapes=[pltpu.VMEM((2, SHARD, 2 * HD), BF16), pltpu.SemaphoreType.DMA],
        compiler_params=params(20),
    )(place, qn, *own, *other, *parts, weight)


def far_kernel(who, place_ref, qn, acc_ref, total_ref, first, second, out_ref, acc, total, shard):
    acc[...] = acc_ref[who]
    total[...] = total_ref[who]
    join(first, second, shard)
    add_shard(place_ref, who, 2, shard, qn.at[who], acc, total)
    out_ref[:, :HD] = acc[...].astype(out_ref.dtype)
    out_ref[:, HD:] = total[...].astype(out_ref.dtype)


def attend_far(who, place, qn, acc, total, first, second):
    return pl.pallas_call(
        functools.partial(far_kernel, who),
        in_specs=[SMEM()] + [VMEM()] * 5,
        out_specs=VMEM(),
        out_shape=jax.ShapeDtypeStruct((QHEADS * QROWS, 2 * HD), BF16 if who else F32),
        scratch_shapes=[
            pltpu.VMEM((QHEADS * QROWS, HD), F32),
            pltpu.VMEM((QHEADS * QROWS, HD), F32),
            pltpu.VMEM((SHARD, 2 * HD), BF16),
        ],
        compiler_params=params(16),
    )(place, qn, acc, total, first, second)


def project_kernel(place_ref, own_ref, other_ref, weight, *refs):
    outs, attn, ordered = refs[:4], refs[4], refs[5]
    z, y, c = place_ref[1], place_ref[2], place_ref[4]
    for h in range(QHEADS):
        at = pl.ds(h * QROWS, QROWS)
        both = own_ref[at, :] + other_ref[at, :].astype(F32)
        whole = jnp.sum(both[:, HD:], axis=1, keepdims=True)
        attn[:, h * HD : (h + 1) * HD] = (both[:, :HD] / whole).astype(BF16)
    for k in range(4):
        for i in range(4):
            over_y = i * 4 + lax.rem(y + k, 4)
            over_z = lax.rem(z + k, 4) * 4 + i
            group = jnp.where(c == 0, over_y, over_z)
            start = pl.multiple_of(group * ROWS, ROWS)
            ordered[pl.ds((k * 4 + i) * ROWS, ROWS), :] = attn[pl.ds(start, ROWS), :]
    for n in range(8):
        part = slice(n * 512, (n + 1) * 512)
        product = jnp.dot(ordered[...], weight[:, part], preferred_element_type=F32)
        product = product.astype(BF16).reshape(GROUPS, ROWS, 512)
        for k in range(4):
            outs[k][:, :, part] = product[k * 4 : (k + 1) * 4]


def project(place, own, other, weight):
    return pl.pallas_call(
        project_kernel,
        in_specs=[SMEM()] + [VMEM()] * 3,
        out_specs=[VMEM()] * 4,
        out_shape=[jax.ShapeDtypeStruct((4, ROWS, WIDTH), BF16)] * 4,
        scratch_shapes=[pltpu.VMEM((QROWS, QHEADS * HD), BF16)] * 2,
        compiler_params=params(16),
    )(place, own, other, weight)


def around(level, step):
    pairs = []
    for z in range(4):
        for y in range(4):
            for x in range(4):
                for c in range(2):
                    to_z, to_y = (z, (y + step) % 4) if c == level else ((z + step) % 4, y)
                    pairs.append((((z * 4 + y) * 4 + x) * 2 + c, ((to_z * 4 + to_y) * 4 + x) * 2 + c))
    return pairs


def sum_kernel(place_ref, *refs):
    parts, outs, held = refs[:4], refs[4:8], refs[8]
    mine = jnp.where(place_ref[4] == 0, place_ref[1], place_ref[2])
    for i in range(4):
        value = parts[0][i].astype(F32)
        for other in parts[1:]:
            value = value + other[i].astype(F32)
        held[i] = value.astype(BF16)
    for k in range(4):
        outs[k][...] = held[lax.rem(mine + k, 4)]


def first_sum(place, parts):
    return pl.pallas_call(
        sum_kernel,
        in_specs=[SMEM()] + [VMEM()] * 4,
        out_specs=[VMEM()] * 4,
        out_shape=[jax.ShapeDtypeStruct((ROWS, WIDTH), BF16)] * 4,
        scratch_shapes=[pltpu.VMEM((4, ROWS, WIDTH), BF16)],
        compiler_params=params(12),
    )(place, *parts)


def query_kernel(q_ref, gain_ref, other_ref, qn, queries, gain, sems):
    copies = (
        pltpu.make_async_copy(gain_ref, gain, sems.at[0]),
        pltpu.make_async_copy(q_ref, queries, sems.at[1]),
    )
    for copy in copies:
        copy.start()
    for copy in copies:
        copy.wait()
    for who, ref in enumerate((queries, other_ref)):
        for h in range(QHEADS):
            head = ref[:, h * HD : (h + 1) * HD].astype(F32)
            qn[who, pl.ds(h * QROWS, QROWS), :] = rms_scale(head, gain[...]).astype(BF16)


def norm_queries(queries, q_gain, other):
    return pl.pallas_call(
        query_kernel,
        in_specs=[HBM()] * 2 + [VMEM()],
        out_specs=VMEM(),
        out_shape=jax.ShapeDtypeStruct((2, QHEADS * QROWS, HD), BF16),
        scratch_shapes=[
            pltpu.VMEM((QROWS, QHEADS * HD), BF16),
            pltpu.VMEM((1, HD), F32),
            pltpu.SemaphoreType.DMA((2,)),
        ],
        compiler_params=params(16),
    )(queries, q_gain, other)


def route_kernel(ids_ref, weights_ref, placing_ref, mixing_ref):
    square = (EXPERTS, EXPERTS)
    expert = lax.broadcasted_iota(jnp.int32, square, 0)
    lane = lax.broadcasted_iota(jnp.int32, square, 1)
    row = lax.broadcasted_iota(jnp.int32, (ROWS, EXPERTS), 0)
    spread = lax.broadcasted_iota(jnp.int32, (ROWS, EXPERTS), 1) % ROWS == row
    spread = jnp.where(spread, 1.0, 0.0).astype(BF16)
    ids = jnp.dot(ids_ref[...].astype(F32).astype(BF16), spread, preferred_element_type=F32)
    ids = ids.astype(jnp.int32)
    weights = jnp.dot(weights_ref[...], spread, preferred_element_type=F32)
    named = jnp.zeros(square, F32)
    value = jnp.zeros(square, F32)
    for k in range(8):
        hit = expert == ids[k : k + 1, :]
        named = jnp.where(hit, 1.0, named)
        value = jnp.where(hit, weights[k : k + 1, :], value)
    earlier = (expert // ROWS == lane // ROWS) & (expert < lane)
    before = jnp.dot(
        named.astype(BF16), jnp.where(earlier, 1.0, 0.0).astype(BF16), preferred_element_type=F32
    )
    lines = (EXPERTS * LINES, EXPERTS)
    line = lax.broadcasted_iota(jnp.int32, lines, 0)
    column = lax.broadcasted_iota(jnp.int32, lines, 1)
    same = (line // SLOTS) % CHUNKS == column // ROWS
    of_expert = line // LINES == column
    for out_ref, held in ((placing_ref, named), (mixing_ref, value)):
        table = jnp.zeros(lines, F32)
        for s in range(SLOTS):
            pick = jnp.where(of_expert & (line % SLOTS == s), 1.0, 0.0).astype(BF16)
            slot = jnp.where(before == s, held, 0.0).astype(BF16)
            table = table + jnp.dot(pick, slot, preferred_element_type=F32)
        table = jnp.where(same, table, 0.0)
        out_ref[...] = (table if out_ref is placing_ref else table.T).astype(BF16)


def route(expert_ids, combine_weight):
    return pl.pallas_call(
        route_kernel,
        in_specs=[VMEM()] * 2,
        out_specs=[VMEM()] * 2,
        out_shape=[
            jax.ShapeDtypeStruct((EXPERTS * LINES, EXPERTS), BF16),
            jax.ShapeDtypeStruct((EXPERTS, EXPERTS * LINES), BF16),
        ],
        compiler_params=params(16),
    )(expert_ids, combine_weight)


def dispatch_kernel(*refs):
    parts, refs = refs[:4], refs[4:]
    residual_ref, gain_ref, placing_ref, hidden_ref, out_ref, pieces = refs
    for n in range(8):
        columns = slice(n * 512, (n + 1) * 512)
        value = residual_ref[:, columns].astype(F32)
        for part in parts:
            value = value + part[:, columns].astype(F32)
        hidden_ref[:, columns] = value
    normed = rms_scale(hidden_ref[...], gain_ref[...]).astype(BF16)
    for k in range(CHUNKS):
        pieces[pl.ds(k * ROWS, ROWS), :] = normed[:, k * PIECE : (k + 1) * PIECE]
    for g in range(8):
        lines = jnp.dot(
            placing_ref[pl.ds(g * GROUP_LINES, GROUP_LINES), :],
            pieces[...],
            preferred_element_type=F32,
        )
        out_ref[pl.ds(g * GROUP, GROUP)] = lines.astype(BF16).reshape(GROUP, LINES, PIECE)


def dispatch(parts, residual, norm_gain, placing):
    return pl.pallas_call(
        dispatch_kernel,
        in_specs=[VMEM()] * 7,
        out_specs=[VMEM()] * 2,
        out_shape=[
            jax.ShapeDtypeStruct((ROWS, WIDTH), F32),
            jax.ShapeDtypeStruct((EXPERTS, LINES, PIECE), BF16),
        ],
        scratch_shapes=[pltpu.VMEM((EXPERTS, PIECE), BF16)],
        compiler_params=params(12),
    )(*parts, residual, norm_gain, placing)


def expert_kernel(
    lines_ref, up_ref, down_ref, out_ref, rows, both, active, back
):
    size = (GROUP_LINES, GROUP_LINES)
    first = lax.broadcasted_iota(jnp.int32, size, 0)
    second = lax.broadcasted_iota(jnp.int32, size, 1)
    span = GROUP * SLOTS

    def held(by_chunk, by_source):
        source = (by_chunk % span) // SLOTS
        line = source * LINES + (by_chunk // span) * SLOTS + by_chunk % SLOTS
        return jnp.where(line == by_source, 1.0, 0.0).astype(BF16)

    gather, scatter = held(first, second), held(second, first)
    for g in range(8):
        group = lines_ref[pl.ds(g * GROUP, GROUP)].reshape(GROUP_LINES, PIECE)
        sorted_lines = jnp.dot(gather, group, preferred_element_type=F32).astype(BF16)
        for k in range(CHUNKS):
            rows[pl.ds(g * span, span), k * PIECE : (k + 1) * PIECE] = sorted_lines[
                k * span : (k + 1) * span, :
            ]
    for n in range(2 * FFE // 256):
        columns = slice(n * 256, (n + 1) * 256)
        both[:, columns] = jnp.dot(rows[...], up_ref[:, columns], preferred_element_type=F32)
    gate = both[:, :FFE]
    active[...] = (gate * jax.nn.sigmoid(gate) * both[:, FFE:]).astype(BF16)
    for k in range(CHUNKS):
        columns = slice(k * PIECE, (k + 1) * PIECE)
        down = jnp.dot(active[...], down_ref[:, columns], preferred_element_type=F32)
        down = down.astype(BF16)
        for g in range(8):
            back[g, pl.ds(k * span, span), :] = down[g * span : (g + 1) * span, :]
    for g in range(8):
        lines = jnp.dot(scatter, back[g], preferred_element_type=F32).astype(BF16)
        out_ref[pl.ds(g * GROUP, GROUP)] = lines.reshape(GROUP, LINES, PIECE)


def experts(lines, gate_up, down):
    return pl.pallas_call(
        expert_kernel,
        in_specs=[VMEM()] * 3,
        out_specs=VMEM(),
        out_shape=jax.ShapeDtypeStruct((EXPERTS, LINES, PIECE), BF16),
        scratch_shapes=[
            pltpu.VMEM((EXPERTS * SLOTS, WIDTH), BF16),
            pltpu.VMEM((EXPERTS * SLOTS, 2 * FFE), F32),
            pltpu.VMEM((EXPERTS * SLOTS, FFE), BF16),
            pltpu.VMEM((8, GROUP_LINES, PIECE), BF16),
        ],
        compiler_params=params(18),
    )(lines, gate_up, down)


def combine_kernel(lines_ref, mixing_ref, hidden_ref, out_ref):
    lines = lines_ref[...].reshape(EXPERTS * LINES, PIECE)
    mixed = jnp.dot(mixing_ref[...], lines, preferred_element_type=F32)
    for k in range(CHUNKS):
        columns = slice(k * PIECE, (k + 1) * PIECE)
        value = hidden_ref[:, columns] + mixed[k * ROWS : (k + 1) * ROWS, :]
        out_ref[:, columns] = value.astype(BF16)


def combine(lines, mixing, hidden):
    return pl.pallas_call(
        combine_kernel,
        in_specs=[VMEM()] * 3,
        out_specs=VMEM(),
        out_shape=jax.ShapeDtypeStruct((ROWS, WIDTH), BF16),
        compiler_params=params(12),
    )(lines, mixing, hidden)


def per_device(
    queries,
    cache,
    new_kv,
    q_gain,
    k_gain,
    out_weight,
    residual,
    norm_gain,
    expert_ids,
    combine_weight,
    prefix_len,
    w_gate_up,
    w_down,
):
    z, y, x, c = (lax.axis_index(name).astype(jnp.int32) for name in ("z", "y", "x", "c"))
    place = jnp.stack([prefix_len[0], z, y, x, c])
    held = functools.partial(pltpu.with_memory_space_constraint, memory_space=pltpu.HBM)
    swap = functools.partial(lax.ppermute, axis_name="c", perm=[(0, 1), (1, 0)])
    other = swap(queries)
    left, right = shift(1), shift(3)
    own = prep(held(cache), held(new_kv), held(k_gain.reshape(1, HD)))
    first_left, second_right = lax.ppermute(own[0], "x", left), lax.ppermute(own[1], "x", right)
    second_left, first_right = lax.ppermute(own[1], "x", left), lax.ppermute(own[0], "x", right)
    qn = norm_queries(held(queries), held(q_gain.reshape(1, HD)), other)
    other = attend_near(1, place, qn, *own)
    first_left, second_right, qn, *other = lax.optimization_barrier(
        (first_left, second_right, qn, *other)
    )
    first, second = lax.ppermute(first_left, "x", left), lax.ppermute(second_right, "x", right)
    mine = attend_near(0, place, qn, *own)
    parts = (first_left, second_left, first_right, second_right)
    acc, total, weight = attend_middle(place, qn, mine, other, parts, held(out_weight))
    far = attend_far(1, place, qn, acc, total, first, second)
    far, acc, total = lax.optimization_barrier((far, acc, total))
    mine = attend_far(0, place, qn, acc, total, first, second)
    everyone = ("z", "y", "x", "c")
    parts = list(project(place, mine, swap(far), weight))
    expert_ids, combine_weight, parts[0] = lax.optimization_barrier(
        (expert_ids.T, combine_weight.T, parts[0])
    )
    placing, mixing = route(expert_ids, combine_weight)
    for level in range(2):
        if level:
            parts = first_sum(place, parts)
        order = (2, 1, 3) if level else (1, 3, 2)
        moved = [lax.ppermute(parts[k], everyone, around(level, k)) for k in order]
        parts = [parts[0], *moved]
    hidden, lines = dispatch(parts, residual, norm_gain.reshape(1, WIDTH), placing)
    lines = lax.all_to_all(lines, everyone, split_axis=0, concat_axis=0, tiled=True)
    lines = experts(lines, w_gate_up[0], w_down[0])
    lines = lax.all_to_all(lines, everyone, split_axis=0, concat_axis=0, tiled=True)
    return combine(lines, mixing, hidden)


def solution(mesh):
    fine = Mesh(mesh.devices.reshape(4, 4, 4, 2), ("z", "y", "x", "c"))
    head, tok = ("z", "y"), ("x", "c")
    placed = (
        P(tok, head),
        P(None, tok, None),
        P(None, tok, None),
        P(),
        P(),
        P(head, None),
        P(tok + head, None),
        P(),
        P(tok + head, None),
        P(tok + head, None),
        P(),
        P(head + tok, None, None),
        P(head + tok, None, None),
    )
    return jax.shard_map(
        per_device, mesh=fine, in_specs=placed, out_specs=P(tok + head, None), check_vma=False
    )
```
